256 devices in a mesh: seq: 32 (over z_hi, x, core), batch: 8 (over z_lo, y).
Axes of the slice: x: 4, y: 4, z: 8 (z_hi: 4, z_lo: 2; z = z_hi * 2 + z_lo), core: 2. Of those that a mesh axis runs over, the one named last changes fastest.
Arguments:
- inputs: bfloat16 [8, 8192, 1024], P('batch', 'seq'), may hold values from -6 to 6
- grad_out: bfloat16 [8, 8192, 1024], P('batch', 'seq'), may hold values from -6 to 6
- spectrum: float32 [2, 64, 256, 1024], P(None, 'seq', None, 'batch'), may hold values from -6 to 6
- first_moment: float32 [2, 64, 256, 1024], P(None, 'seq', None, 'batch'), may hold values from -2 to 2
- second_moment: float32 [2, 64, 256, 1024], P(None, 'seq', None, 'batch'), may hold values from 0.1 to 4
Outputs:
- new_spectrum: float32 [2, 64, 256, 1024], P(None, 'seq', None, 'batch')
- new_first: float32 [2, 64, 256, 1024], P(None, 'seq', None, 'batch')
- new_second: float32 [2, 64, 256, 1024], P(None, 'seq', None, 'batch')
- filtered: bfloat16 [8, 8192, 1024], P('batch', 'seq')
The draws below stay inside these ranges and needn't reach their ends.
All inputs are finite; a program needn't handle non-finite values.
Results may differ from the reference program's by a relative error of at most 0.0055.
Values may be sent and summed in bfloat16 or wider, within the bound.
A program may use at most 64 MiB of HBM per device.

```python
import math
import jax
import jax.numpy as jnp
from jax import lax

H = 1024
SEQ_DEV = 256
SEQ = 8192
BATCH = 8
FREQ_OUTER = 64


def strengthened(array, own_key, source, target, blocks, factor):
    owner, partner = [(jnp.arange(array.shape[position]) // (array.shape[position] // blocks)).reshape([-1 if axis == position else 1 for axis in range(array.ndim)]) for position in (source, target)]
    chosen = jax.random.permutation(own_key, blocks)[partner]
    strong = (owner == chosen) | (owner == (partner + blocks // 2) % blocks)
    return jnp.where(strong, factor * array, array)


def block_levels(rng, dims, cuts, low, high):
    def one(axis_at, parts):
        heights = jax.random.uniform(jax.random.fold_in(jax.random.fold_in(rng, 6), axis_at), (parts,), jnp.float32, low / len(cuts), high / len(cuts))
        return jnp.repeat(jnp.exp(heights), dims[axis_at] // parts).reshape((-1,) + (1,) * (len(dims) - axis_at - 1))

    loudness = one(*cuts[0])
    for cut in cuts[1:]:
        loudness = loudness * one(*cut)
    return loudness


def gaussian(rng, extent, scale, bound, cuts=(), kind=jnp.bfloat16):
    values = scale * jax.random.normal(rng, extent, jnp.float32)
    if cuts:
        values = values * block_levels(rng, extent, cuts, -0.22, 0.18)
    return jnp.clip(values, -bound, bound).astype(kind)


def bell_draw_with(own_key, shape, spread, limit, pieces, heavy, held_as=jnp.bfloat16):
    array = spread * jax.random.normal(own_key, shape, jnp.float32)
    if pieces:
        array = array * block_levels(own_key, shape, pieces, -0.22, 0.18)
    return jnp.clip(strengthened(array, jax.random.fold_in(own_key, 3), *heavy), -limit, limit).astype(held_as)


def setup_inputs(seed: int = 0) -> dict:
    streams_of = jax.random.split(jax.random.key(seed), 6)
    return {
        "inputs": gaussian(streams_of[0], (BATCH, SEQ, H), 1.0, 6.0, ((0, 8), (1, 32))),
        "grad_out": bell_draw_with(streams_of[1], (BATCH, SEQ, H), 1.0, 6.0, ((0, 8), (1, 32)), (0, 2, 8, 2.0)),
        "spectrum": gaussian(streams_of[2], (2, FREQ_OUTER, SEQ_DEV, H), 1.0, 6.0, ((1, 32), (3, 8)), jnp.float32),
        "first_moment": gaussian(streams_of[3], (2, FREQ_OUTER, SEQ_DEV, H), 0.3, 2.0, ((1, 32), (3, 8)), jnp.float32),
        "second_moment": jnp.clip(jnp.exp(math.log(4.0) - 3.6888794 * jax.random.uniform(streams_of[4], (2, FREQ_OUTER, SEQ_DEV, H), jnp.float32) ** block_levels(streams_of[4], (2, FREQ_OUTER, SEQ_DEV, H), ((1, 32), (3, 8)), -0.2, 0.2)), 0.1, 4.0),
    }


def spectra(sequence):
    padded = jnp.concatenate([sequence.astype(jnp.float32), jnp.zeros((SEQ, H), jnp.float32)], axis=0)
    transform = jnp.fft.fft(padded, axis=0)
    return transform.reshape(SEQ_DEV, FREQ_OUTER, H).transpose(1, 0, 2)

def reference(inputs, grad_out, spectrum, first_moment, second_moment):
    full_length = 2 * SEQ

    def accumulate(carry, pair):
        signal_spec = spectra(pair[0])
        grad_spec = spectra(pair[1])
        product = jnp.conj(signal_spec) * grad_spec
        term = jnp.stack([jnp.real(product), jnp.imag(product)]) / full_length
        return (carry + term, None)
    start_grad = jnp.zeros((2, FREQ_OUTER, SEQ_DEV, H), jnp.float32)
    grad, unused = lax.scan(accumulate, start_grad, (inputs, grad_out))
    new_first = 0.9 * first_moment + 0.1 * grad
    new_second = 0.99 * second_moment + 0.01 * grad * grad
    new_spectrum = spectrum - 0.5 * jnp.tanh(new_first / (jnp.sqrt(new_second) + 1e-06))
    complex_filter = new_spectrum[0] + 1j * new_spectrum[1]

    def reapply(sequence):
        product = spectra(sequence) * complex_filter
        ordered = product.transpose(1, 0, 2).reshape(full_length, H)
        result = jnp.real(jnp.fft.ifft(ordered, axis=0))[:SEQ]
        return result.astype(jnp.bfloat16)
    filtered = lax.map(reapply, inputs)
    return (new_spectrum, new_first, new_second, filtered)
```

```python
import math

import jax
import jax.numpy as jnp
import ml_dtypes
import numpy as np
from jax import lax
from jax.experimental import pallas as pl
from jax.experimental.pallas import tpu as pltpu
from jax.sharding import PartitionSpec as P

S = 32
B = 8
C = 256
N = 2 * S * C
LANES = 128
K4 = LANES // S
SLOTS = 40
ROWS = K4 * SLOTS
BF, F32 = jnp.bfloat16, jnp.float32


def two_parts(x):
    high = x.astype(ml_dtypes.bfloat16)
    low = (x - high.astype(np.float64)).astype(ml_dtypes.bfloat16)
    return high, low


def constants():
    pack = np.zeros((S, 2, 2, K4, 2, 2, LANES), np.float32)
    for s in range(S):
        for t in range(2):
            for h in range(2):
                for k in range(K4):
                    pack[s, t, h, k, t, h, K4 * s + k] = 1
    pack = pack.reshape(S * 16, 512)
    slot = np.arange(SLOTS)[:, None]
    used = (slot <= S).astype(np.float64)
    a = np.arange(S)[None, :]
    outer = 2 * math.pi * (slot * a % (2 * S)) / (2 * S)
    f = np.concatenate([np.cos(outer) * used, -np.sin(outer) * used], 0)
    f_high, f_low = two_parts(f)
    forward_outer = np.concatenate([f_high, f_low], 1)
    c = np.arange(C)[None, :]
    twist = 2 * math.pi * (slot * c % N) / N
    twist = np.stack([np.cos(twist) * used, np.sin(twist) * used]).astype(np.float32)
    inner = 2 * math.pi * (c.T * c % C) / C
    cos, sin = np.cos(inner), np.sin(inner)
    w = np.block([[cos, -sin], [sin, cos]])
    w_high, w_low = two_parts(w)
    l_high, l_low = two_parts(f.T / N)
    inverse_outer = np.concatenate([l_high, l_low, l_high], 1)
    spread = np.zeros((S, 2, 2, K4, 2, K4, SLOTS), np.float32)
    order = np.zeros((S, 2, 2, K4, 2, 2, LANES), np.float32)
    for s in range(S):
        for ri in range(2):
            for j2 in range(2):
                for k in range(K4):
                    j = 2 * s + j2
                    spread[s, ri, j2, k, ri, k, j if s < S // 2 else 2 * S - j] = 1
                    order[s, ri, j2, k, ri, j2, K4 * s + k] = 1
    spread = spread.reshape(S * 16, 2 * ROWS)
    order = order.reshape(S * 16, 4 * LANES)
    unpack = np.zeros((S, 2, K4, 2, LANES), np.float32)
    for s in range(S):
        for h in range(2):
            for k in range(K4):
                unpack[s, h, k, h, K4 * s + k] = 1
    unpack = unpack.reshape(S * 8, 2 * LANES)
    small = lambda x: x.astype(ml_dtypes.bfloat16)
    return dict(
        pack=small(pack),
        fo=small(forward_outer),
        wh=w_high,
        wl=w_low,
        tw=twist,
        spread=small(spread),
        orderT=small(order.T),
        order=small(order),
        spreadT=small(spread.T),
        io=small(inverse_outer),
        unpack=small(unpack),
    )


NAMES = ("pack", "fo", "wh", "wl", "tw", "spread", "orderT", "order", "spreadT", "io", "unpack")


def dot(x, y):
    return lax.dot_general(x, y, (((1,), (0,)), ((), ())), preferred_element_type=F32)


def dot_t(x, y):
    return lax.dot_general(x, y, (((1,), (1,)), ((), ())), preferred_element_type=F32)


def split(x):
    high = x.astype(BF)
    return high, (x - high.astype(F32)).astype(BF)


def pack_block(x, g, pack):
    cols = jnp.concatenate([x[:LANES], x[LANES:], g[:LANES], g[LANES:]], axis=1)
    return dot_t(pack, cols).astype(BF).reshape(S, 16, LANES)


def forward(d, fo, tc, ts, wh, wl):
    dt = jnp.swapaxes(d.astype(F32), 0, 1).astype(BF)
    cols = [dt[8 * t + 4 * h + k] for t in range(2) for k in range(K4) for h in range(2)]
    dc = jnp.concatenate(cols, axis=1)
    z = dot(fo, jnp.concatenate([dc, dc], axis=0))
    re, im = [], []
    for i in range(2 * K4):
        zr = z[:SLOTS, C * i : C * i + C]
        zi = z[SLOTS:, C * i : C * i + C]
        re.append(zr * tc + zi * ts)
        im.append(zi * tc - zr * ts)
    rows = jnp.concatenate([jnp.concatenate(re, axis=0), jnp.concatenate(im, axis=0)], axis=1)
    high, low = split(rows)
    out = dot(high, wh) + dot(low, wh) + dot(high, wl)
    return out[:ROWS], out[ROWS:]


def product(x, g):
    xr, xi, gr, gi = x[:, :C], x[:, C:], g[:, :C], g[:, C:]
    return jnp.concatenate([xr * gr + xi * gi, xr * gi - xi * gr], axis=1)


def spread_grad(total, spread):
    small = (total * (1.0 / N)).astype(BF)
    cols = jnp.concatenate([small[:, :C], small[:, C:]], axis=0)
    return dot(spread, cols).astype(BF)


def turn(flip):
    row = lax.broadcasted_iota(jnp.int32, (C, C), 0)
    col = lax.broadcasted_iota(jnp.int32, (C, C), 1)
    return jnp.where(col == jnp.where(flip, C - 1 - row, row), 1.0, 0.0).astype(BF)


def own_grad(cols, order_t, r):
    return dot_t(r, dot(order_t, cols).astype(BF))


def spread_filter(k, order, r):
    return dot_t(order, dot(r, k.astype(BF)).astype(BF)).astype(BF)


def inverse(x, kr, ki, io, tc, ts, wh, wl):
    xr, xi = x[:, :C], x[:, C:]
    high, low = split(jnp.concatenate([xr * kr - xi * ki, xr * ki + xi * kr], axis=1))
    o = dot_t(high, wh) + dot_t(low, wh) + dot_t(high, wl)
    cols = []
    for k in range(K4):
        zr = o[SLOTS * k : SLOTS * (k + 1), :C]
        zi = o[SLOTS * k : SLOTS * (k + 1), C:]
        cols.append(jnp.concatenate([zr * tc - zi * ts, zr * ts + zi * tc], axis=0))
    vh, vl = split(jnp.concatenate(cols, axis=1))
    y = dot(io, jnp.concatenate([vh, vh, vl], axis=0))
    parts = [y[:, C * k + LANES * h : C * k + LANES * (h + 1)] for h in range(2) for k in range(K4)]
    return jnp.swapaxes(jnp.stack(parts, axis=0), 0, 1).astype(BF)


def unpack_block(y, unpack):
    row = lax.broadcasted_iota(jnp.int32, (LANES, LANES), 0)
    col = lax.broadcasted_iota(jnp.int32, (LANES, LANES), 1)
    eye = jnp.where(row == col, 1.0, 0.0).astype(BF)
    return dot(dot_t(eye, y).astype(BF), unpack).astype(BF)


def kernel(
    x_hbm, g_hbm, k_hbm, f_hbm, s_hbm, *rest
):
    consts_hbm = rest[: len(NAMES)]
    nk_hbm, nf_hbm, ns_hbm, y_hbm = rest[len(NAMES) : len(NAMES) + 4]
    rest = rest[len(NAMES) + 4 :]
    consts = dict(zip(NAMES, rest[: len(NAMES)]))
    (
        x_v, g_v, k_v, f_v, s_v, y_v,
        xs, xr, spec, total, gs, gr, ks, kr, kc, ys, yr,
        in_sem, const_sem, state_sem, out_sem,
        xs_sem, xr_sem, gs_sem, gr_sem, ks_sem, kr_sem, ys_sem, yr_sem,
    ) = rest[len(NAMES) :]
    me = lax.axis_index("seq")
    mb = lax.axis_index("batch")

    loads = [
        pltpu.make_async_copy(x_hbm, x_v, in_sem.at[0]),
        pltpu.make_async_copy(g_hbm, g_v, in_sem.at[1]),
    ]
    const_loads = [
        pltpu.make_async_copy(h, consts[name], const_sem.at[i])
        for i, (name, h) in enumerate(zip(NAMES, consts_hbm))
    ]
    state_loads = [
        pltpu.make_async_copy(k_hbm, k_v, state_sem.at[0]),
        pltpu.make_async_copy(f_hbm, f_v, state_sem.at[1]),
        pltpu.make_async_copy(s_hbm, s_v, state_sem.at[2]),
    ]
    for copy in loads + const_loads + state_loads:
        copy.start()
    for copy in loads + const_loads[:1]:
        copy.wait()

    def send_block(d, first):
        to = lax.rem(mb + d, B)
        cols = pl.ds(pl.multiple_of(to * LANES, LANES), LANES)
        xs[to] = pack_block(x_v[:, cols], g_v[:, cols], consts["pack"][...])

        def one(e, carry):
            there = lax.rem(me + e, S)
            pltpu.make_async_remote_copy(
                src_ref=xs.at[to, there],
                dst_ref=xr.at[mb, me],
                send_sem=xs_sem.at[d],
                recv_sem=xr_sem.at[mb],
                device_id={"seq": there, "batch": to},
                device_id_type=pl.DeviceIdType.MESH,
            ).start()
            return carry

        lax.fori_loop(first, S, one, 0)

    send_block(0, 1)
    pltpu.make_async_copy(xs.at[mb, me], xr.at[mb, me], xr_sem.at[mb]).start()

    def send_step(d, carry):
        send_block(d, 0)
        return carry

    lax.fori_loop(1, B, send_step, 0)
    for copy in const_loads[1:]:
        copy.wait()

    total[...] = jnp.zeros_like(total)

    def forward_step(d, carry):
        q = lax.rem(mb + B - d, B)
        pltpu.make_async_copy(xr.at[q], xr.at[q], xr_sem.at[q]).wait()
        sx, sg = forward(
            xr[q], consts["fo"][...], consts["tw"][0], consts["tw"][1], consts["wh"][...], consts["wl"][...]
        )
        spec[q] = sx
        total[...] += product(sx, sg)
        return carry

    lax.fori_loop(0, B, forward_step, 0)

    def exchange(sent, landed, send_sem, recv_sem):
        pltpu.make_async_copy(sent.at[me], landed.at[me], recv_sem).start()

        def one(e, carry):
            there = lax.rem(me + e, S)
            pltpu.make_async_remote_copy(
                src_ref=sent.at[there],
                dst_ref=landed.at[me],
                send_sem=send_sem,
                recv_sem=recv_sem,
                device_id={"seq": there, "batch": mb},
                device_id_type=pl.DeviceIdType.MESH,
            ).start()
            return carry

        lax.fori_loop(1, S, one, 0)

    def store_halves(ref, value):
        for h in range(2):
            ref[:, h] = value[:, LANES * h : LANES * (h + 1)].reshape(S, 16, LANES)

    def halves(ref):
        return jnp.concatenate([ref[:, h].reshape(S * 16, LANES) for h in range(2)], axis=1)

    store_halves(gs, spread_grad(total[...], consts["spread"][...]))
    exchange(gs, gr, gs_sem, gr_sem)
    for copy in state_loads:
        copy.wait()
    flip = me >= S // 2
    r = turn(flip)
    sign = jnp.where(flip, -1.0, 1.0).astype(F32)
    pltpu.make_async_copy(gr, gr, gr_sem).wait()

    grad = own_grad(halves(gr), consts["orderT"][...], r)
    cols = []
    for ri in range(2):
        for j2 in range(2):
            at = (2 * ri + j2) * LANES
            part = grad[:, at : at + LANES]
            if ri == 1:
                part = part * sign
            first = 0.9 * f_v[ri, j2] + 0.1 * part
            second = 0.99 * s_v[ri, j2] + 0.01 * part * part
            new = k_v[ri, j2] - 0.5 * jnp.tanh(first / (jnp.sqrt(second) + 1e-6))
            f_v[ri, j2] = first
            s_v[ri, j2] = second
            k_v[ri, j2] = new
            cols.append(new * sign if ri == 1 else new)
    store_halves(ks, spread_filter(jnp.concatenate(cols, axis=1), consts["order"][...], r))
    exchange(ks, kr, ks_sem, kr_sem)
    stores = [
        pltpu.make_async_copy(k_v, nk_hbm, out_sem.at[0]),
        pltpu.make_async_copy(f_v, nf_hbm, out_sem.at[1]),
        pltpu.make_async_copy(s_v, ns_hbm, out_sem.at[2]),
    ]
    for copy in stores:
        copy.start()
    pltpu.make_async_copy(kr, kr, kr_sem).wait()
    kc[...] = dot(consts["spreadT"][...], halves(kr))

    def inverse_block(d, first):
        q = lax.rem(mb + d, B)
        ys[q] = inverse(
            spec[q], kc[:ROWS], kc[ROWS:], consts["io"][...], consts["tw"][0], consts["tw"][1],
            consts["wh"][...], consts["wl"][...],
        )

        def one(e, carry):
            there = lax.rem(me + e, S)
            pltpu.make_async_remote_copy(
                src_ref=ys.at[q, there],
                dst_ref=yr.at[mb, me],
                send_sem=ys_sem.at[d],
                recv_sem=yr_sem.at[mb],
                device_id={"seq": there, "batch": q},
                device_id_type=pl.DeviceIdType.MESH,
            ).start()
            return carry

        lax.fori_loop(first, S, one, 0)

    inverse_block(0, 1)
    pltpu.make_async_copy(ys.at[mb, me], yr.at[mb, me], yr_sem.at[mb]).start()

    def inverse_step(d, carry):
        inverse_block(d, 0)
        return carry

    lax.fori_loop(1, B, inverse_step, 0)

    def finish_step(d, carry):
        came = lax.rem(mb + B - d, B)
        pltpu.make_async_copy(yr.at[came], yr.at[came], yr_sem.at[came]).wait()
        rows = yr[came].astype(F32).reshape(S * 8, LANES).astype(BF)
        o = unpack_block(rows, consts["unpack"][...])
        at = pl.ds(pl.multiple_of(came * LANES, LANES), LANES)
        y_v[:LANES, at] = o[:, :LANES]
        y_v[LANES:, at] = o[:, LANES:]
        return carry

    lax.fori_loop(0, B, finish_step, 0)
    last = pltpu.make_async_copy(y_v, y_hbm, out_sem.at[3])
    last.start()

    def drain(d, carry):
        pltpu.make_async_copy(xs.at[0], xs.at[0], xs_sem.at[d]).wait()
        pltpu.make_async_copy(ys.at[0], ys.at[0], ys_sem.at[d]).wait()
        return carry

    for buffer, sem in ((xs.at[0], xs_sem.at[0]), (gs, gs_sem), (ks, ks_sem), (ys.at[0], ys_sem.at[0])):
        part = buffer.at[pl.ds(0, S - 1)]
        pltpu.make_async_copy(part, part, sem).wait()
    lax.fori_loop(1, B, drain, 0)
    for copy in stores:
        copy.wait()
    last.wait()


def per_device(inputs, grad_out, spectrum, first_moment, second_moment):
    table = constants()
    consts = [jnp.asarray(table[name]) for name in NAMES]
    any_spec = pl.BlockSpec(memory_space=pl.ANY)
    state = (2, 2, C, LANES)
    wide = (C, B * LANES)
    dma = pltpu.SemaphoreType.DMA
    scratch = [pltpu.VMEM(v.shape, v.dtype) for v in consts]
    scratch += [
        pltpu.VMEM(wide, BF),
        pltpu.VMEM(wide, BF),
        pltpu.VMEM(state, F32),
        pltpu.VMEM(state, F32),
        pltpu.VMEM(state, F32),
        pltpu.VMEM(wide, BF),
        pltpu.VMEM((B, S, 16, LANES), BF),
        pltpu.VMEM((B, S, 16, LANES), BF),
        pltpu.VMEM((B, ROWS, 2 * C), F32),
        pltpu.VMEM((ROWS, 2 * C), F32),
        pltpu.VMEM((S, 2, 16, LANES), BF),
        pltpu.VMEM((S, 2, 16, LANES), BF),
        pltpu.VMEM((S, 2, 16, LANES), BF),
        pltpu.VMEM((S, 2, 16, LANES), BF),
        pltpu.VMEM((2 * ROWS, C), F32),
        pltpu.VMEM((B, S, 8, LANES), BF),
        pltpu.VMEM((B, S, 8, LANES), BF),
        dma((2,)),
        dma((len(NAMES),)),
        dma((3,)),
        dma((4,)),
        dma((B,)),
        dma((B,)),
        dma,
        dma,
        dma,
        dma,
        dma((B,)),
        dma((B,)),
    ]
    nk, nf, ns, y = pl.pallas_call(
        kernel,
        out_shape=(
            jax.ShapeDtypeStruct(state, F32),
            jax.ShapeDtypeStruct(state, F32),
            jax.ShapeDtypeStruct(state, F32),
            jax.ShapeDtypeStruct(wide, BF),
        ),
        in_specs=[any_spec] * (5 + len(NAMES)),
        out_specs=(any_spec,) * 4,
        scratch_shapes=scratch,
        compiler_params=pltpu.CompilerParams(
            has_side_effects=True, vmem_limit_bytes=48 * 1024 * 1024
        ),
        name="long_convolution_update",
    )(inputs[0], grad_out[0], spectrum, first_moment, second_moment, *consts)
    return nk, nf, ns, y[None]


def solution(mesh):
    state = P(None, "seq", None, "batch")
    rows = P("batch", "seq", None)
    return jax.shard_map(
        per_device,
        mesh=mesh,
        in_specs=(rows, rows, state, state, state),
        out_specs=(state, state, state, rows),
        check_vma=False,
    )
```

```python
import math

import jax
import jax.numpy as jnp
from jax import lax
from jax.experimental import pallas as pl
from jax.experimental.pallas import tpu as pltpu
from jax.sharding import PartitionSpec as P

S = 32
B = 8
C = 256
N = 2 * S * C
LANES = 128
K4 = LANES // S
SLOTS = 40
ROWS = K4 * SLOTS
BF, F32 = jnp.bfloat16, jnp.float32


def iota(shape, dim):
    return lax.broadcasted_iota(jnp.int32, shape, dim)


def selection(rows, cols, target, transposed=False):
    if transposed:
        return jnp.where(iota((cols, rows), 0) == target(iota((1, rows), 1)), 1.0, 0.0).astype(BF)
    return jnp.where(iota((rows, cols), 1) == target(iota((rows, 1), 0)), 1.0, 0.0).astype(BF)


def pack_at(row):
    s, th, k = row >> 4, (row >> 2) & 3, row & 3
    return th * LANES + K4 * s + k


def spread_at(row):
    s, ri, j2, k = row >> 4, (row >> 3) & 1, (row >> 2) & 1, row & 3
    j = 2 * s + j2
    return ri * ROWS + k * SLOTS + jnp.where(s < S // 2, j, 2 * S - j)


def order_at(row):
    s, rj, k = row >> 4, (row >> 2) & 3, row & 3
    return rj * LANES + K4 * s + k


def unpack_at(row):
    s, h, k = row >> 3, (row >> 2) & 1, row & 3
    return h * LANES + K4 * s + k


def make_forward_outer():
    slot = iota((SLOTS, S), 0)
    used = jnp.where(slot <= S, 1.0, 0.0)
    angle = ((slot * iota((SLOTS, S), 1)) & (2 * S - 1)).astype(F32) * (math.pi / S)
    high, low = split(jnp.concatenate([jnp.cos(angle) * used, -jnp.sin(angle) * used], axis=0))
    return jnp.concatenate([high, low], axis=1)


def make_inverse_outer():
    slot = iota((S, SLOTS), 1)
    used = jnp.where(slot <= S, 1.0 / N, 0.0)
    angle = ((slot * iota((S, SLOTS), 0)) & (2 * S - 1)).astype(F32) * (math.pi / S)
    high, low = split(jnp.concatenate([jnp.cos(angle) * used, -jnp.sin(angle) * used], axis=1))
    return jnp.concatenate([high, low, high], axis=1)


def make_twist(ref):
    angle = (iota((SLOTS, C), 0) * iota((SLOTS, C), 1)).astype(F32) * (2 * math.pi / N)
    ref[0] = jnp.cos(angle)
    ref[1] = jnp.sin(angle)


def make_inner(high_ref, low_ref):
    angle = ((iota((C, C), 0) * iota((C, C), 1)) & (C - 1)).astype(F32) * (2 * math.pi / C)
    for x, places in ((jnp.cos(angle), ((0, 0, 1), (1, 1, 1))), (jnp.sin(angle), ((1, 0, 1), (0, 1, -1)))):
        high, low = split(x)
        for i, j, sign in places:
            at = (pl.ds(C * i, C), pl.ds(C * j, C))
            high_ref[at] = high if sign > 0 else -high
            low_ref[at] = low if sign > 0 else -low


CONSTANTS = dict(
    pack=((512, 512), BF),
    fo=((2 * SLOTS, 2 * S), BF),
    wh=((2 * C, 2 * C), BF),
    wl=((2 * C, 2 * C), BF),
    tw=((2, SLOTS, C), F32),
    spread=((512, 2 * ROWS), BF),
    order_t=((512, 512), BF),
    order=((512, 512), BF),
    spread_t=((2 * ROWS, 512), BF),
    io=((S, 6 * SLOTS), BF),
    unpack=((256, 256), BF),
)


def dot(x, y):
    return lax.dot_general(x, y, (((1,), (0,)), ((), ())), preferred_element_type=F32)


def dot_t(x, y):
    return lax.dot_general(x, y, (((1,), (1,)), ((), ())), preferred_element_type=F32)


def split(x):
    high = x.astype(BF)
    return high, (x - high.astype(F32)).astype(BF)


def pack_block(x, g, pack):
    cols = jnp.concatenate([x[:LANES], x[LANES:], g[:LANES], g[LANES:]], axis=1)
    return dot_t(pack, cols).astype(BF).reshape(S, 16, LANES)


def forward(d, fo, tc, ts, wh, wl):
    dt = jnp.swapaxes(d.astype(F32), 0, 1).astype(BF)
    cols = [dt[8 * t + 4 * h + k] for t in range(2) for k in range(K4) for h in range(2)]
    dc = jnp.concatenate(cols, axis=1)
    z = dot(fo, jnp.concatenate([dc, dc], axis=0))
    re, im = [], []
    for i in range(2 * K4):
        zr = z[:SLOTS, C * i : C * i + C]
        zi = z[SLOTS:, C * i : C * i + C]
        re.append(zr * tc + zi * ts)
        im.append(zi * tc - zr * ts)
    rows = jnp.concatenate([jnp.concatenate(re, axis=0), jnp.concatenate(im, axis=0)], axis=1)
    high, low = split(rows)
    out = dot(high, wh) + dot(low, wh) + dot(high, wl)
    return out[:ROWS], out[ROWS:]


def product(x, g):
    xr, xi, gr, gi = x[:, :C], x[:, C:], g[:, :C], g[:, C:]
    return jnp.concatenate([xr * gr + xi * gi, xr * gi - xi * gr], axis=1)


def spread_grad(total, spread):
    small = (total * (1.0 / N)).astype(BF)
    cols = jnp.concatenate([small[:, :C], small[:, C:]], axis=0)
    return dot(spread, cols).astype(BF)


def turn(flip):
    row = lax.broadcasted_iota(jnp.int32, (C, C), 0)
    col = lax.broadcasted_iota(jnp.int32, (C, C), 1)
    return jnp.where(col == jnp.where(flip, C - 1 - row, row), 1.0, 0.0).astype(BF)


def own_grad(cols, order_t, r):
    return dot_t(r, dot(order_t, cols).astype(BF))


def spread_filter(k, order, r):
    return dot_t(order, dot(r, k.astype(BF)).astype(BF)).astype(BF)


def inverse(x, kr, ki, io, tc, ts, wh, wl):
    xr, xi = x[:, :C], x[:, C:]
    high, low = split(jnp.concatenate([xr * kr - xi * ki, xr * ki + xi * kr], axis=1))
    o = dot_t(high, wh) + dot_t(low, wh) + dot_t(high, wl)
    cols = []
    for k in range(K4):
        zr = o[SLOTS * k : SLOTS * (k + 1), :C]
        zi = o[SLOTS * k : SLOTS * (k + 1), C:]
        cols.append(jnp.concatenate([zr * tc - zi * ts, zr * ts + zi * tc], axis=0))
    vh, vl = split(jnp.concatenate(cols, axis=1))
    y = dot(io, jnp.concatenate([vh, vh, vl], axis=0))
    parts = [y[:, C * k + LANES * h : C * k + LANES * (h + 1)] for h in range(2) for k in range(K4)]
    return jnp.swapaxes(jnp.stack(parts, axis=0), 0, 1).astype(BF)


def unpack_block(y, unpack):
    row = lax.broadcasted_iota(jnp.int32, (LANES, LANES), 0)
    col = lax.broadcasted_iota(jnp.int32, (LANES, LANES), 1)
    eye = jnp.where(row == col, 1.0, 0.0).astype(BF)
    return dot(dot_t(eye, y).astype(BF), unpack).astype(BF)


def kernel(
    x_hbm, g_hbm, k_hbm, f_hbm, s_hbm, *rest
):
    nk_hbm, nf_hbm, ns_hbm, y_hbm = rest[:4]
    rest = rest[4:]
    consts = dict(zip(CONSTANTS, rest[: len(CONSTANTS)]))
    (
        x_v, g_v, k_v, f_v, s_v, y_v,
        xs, xr, spec, total, gs, gr, ks, kr, kc, ys, yr,
        group_sem, in_sem, state_sem, out_sem,
        xs_sem, xr_sem, gs_sem, gr_sem, ks_sem, kr_sem, ys_sem, yr_sem,
    ) = rest[len(CONSTANTS) :]
    me = lax.axis_index("seq")
    mb = lax.axis_index("batch")

    barrier = pltpu.get_barrier_semaphore()

    def greet_seq(e, carry):
        pl.semaphore_signal(
            barrier, inc=1, device_id={"seq": lax.rem(me + e, S), "batch": mb}, device_id_type=pl.DeviceIdType.MESH
        )
        return carry

    def greet_batch(d, carry):
        pl.semaphore_signal(
            barrier, inc=1, device_id={"seq": me, "batch": lax.rem(mb + d, B)}, device_id_type=pl.DeviceIdType.MESH
        )
        return carry

    def greet_groups(d, carry):
        pl.semaphore_signal(
            group_sem.at[mb],
            inc=1,
            device_id={"seq": me, "batch": lax.rem(mb + d, B)},
            device_id_type=pl.DeviceIdType.MESH,
        )
        return carry

    lax.fori_loop(1, S, greet_seq, 0)
    lax.fori_loop(1, B, greet_batch, 0)

    loads = [
        pltpu.make_async_copy(x_hbm, x_v, in_sem.at[0]),
        pltpu.make_async_copy(g_hbm, g_v, in_sem.at[1]),
    ]
    state_loads = [
        pltpu.make_async_copy(k_hbm, k_v, state_sem.at[0]),
        pltpu.make_async_copy(f_hbm, f_v, state_sem.at[1]),
        pltpu.make_async_copy(s_hbm, s_v, state_sem.at[2]),
    ]
    for copy in loads + state_loads:
        copy.start()
    consts["pack"][...] = selection(512, 512, pack_at)
    for copy in loads:
        copy.wait()

    pl.semaphore_wait(barrier, S - 1 + B - 1)
    lax.fori_loop(1, B, greet_groups, 0)

    def send_block(d, first, own=False):
        to = lax.rem(mb + d, B)
        cols = pl.ds(pl.multiple_of(to * LANES, LANES), LANES)
        xs[to] = pack_block(x_v[:, cols], g_v[:, cols], consts["pack"][...])
        if not own:
            pl.semaphore_wait(group_sem.at[to], 1)

        def one(e, carry):
            there = lax.rem(me + e, S)
            pltpu.make_async_remote_copy(
                src_ref=xs.at[to, there],
                dst_ref=xr.at[mb, me],
                send_sem=xs_sem.at[d],
                recv_sem=xr_sem.at[mb],
                device_id={"seq": there, "batch": to},
                device_id_type=pl.DeviceIdType.MESH,
            ).start()
            return carry

        lax.fori_loop(first, S, one, 0)

    send_block(0, 1, True)
    pltpu.make_async_copy(xs.at[mb, me], xr.at[mb, me], xr_sem.at[mb]).start()

    def send_step(d, carry):
        send_block(d, 0)
        return carry

    lax.fori_loop(1, B, send_step, 0)
    consts["fo"][...] = make_forward_outer()
    make_twist(consts["tw"])
    make_inner(consts["wh"], consts["wl"])
    consts["spread"][...] = selection(512, 2 * ROWS, spread_at)
    consts["spread_t"][...] = selection(512, 2 * ROWS, spread_at, True)
    consts["order"][...] = selection(512, 512, order_at)
    consts["order_t"][...] = selection(512, 512, order_at, True)
    consts["io"][...] = make_inverse_outer()
    consts["unpack"][...] = selection(256, 256, unpack_at)

    total[...] = jnp.zeros_like(total)

    def forward_step(d, carry):
        q = lax.rem(mb + B - d, B)
        pltpu.make_async_copy(xr.at[q], xr.at[q], xr_sem.at[q]).wait()
        sx, sg = forward(
            xr[q], consts["fo"][...], consts["tw"][0], consts["tw"][1], consts["wh"][...], consts["wl"][...]
        )
        spec[q] = sx
        total[...] += product(sx, sg)
        return carry

    lax.fori_loop(0, B, forward_step, 0)

    def exchange(sent, landed, send_sem, recv_sem):
        pltpu.make_async_copy(sent.at[me], landed.at[me], recv_sem).start()

        def one(e, carry):
            there = lax.rem(me + e, S)
            pltpu.make_async_remote_copy(
                src_ref=sent.at[there],
                dst_ref=landed.at[me],
                send_sem=send_sem,
                recv_sem=recv_sem,
                device_id={"seq": there, "batch": mb},
                device_id_type=pl.DeviceIdType.MESH,
            ).start()
            return carry

        lax.fori_loop(1, S, one, 0)

    def store_halves(ref, value):
        for h in range(2):
            ref[:, h] = value[:, LANES * h : LANES * (h + 1)].reshape(S, 16, LANES)

    def halves(ref):
        return jnp.concatenate([ref[:, h].reshape(S * 16, LANES) for h in range(2)], axis=1)

    store_halves(gs, spread_grad(total[...], consts["spread"][...]))
    exchange(gs, gr, gs_sem, gr_sem)
    for copy in state_loads:
        copy.wait()
    flip = me >= S // 2
    r = turn(flip)
    sign = jnp.where(flip, -1.0, 1.0).astype(F32)
    pltpu.make_async_copy(gr, gr, gr_sem).wait()

    grad = own_grad(halves(gr), consts["order_t"][...], r)
    cols = []
    for ri in range(2):
        for j2 in range(2):
            at = (2 * ri + j2) * LANES
            part = grad[:, at : at + LANES]
            if ri == 1:
                part = part * sign
            first = 0.9 * f_v[ri, j2] + 0.1 * part
            second = 0.99 * s_v[ri, j2] + 0.01 * part * part
            new = k_v[ri, j2] - 0.5 * jnp.tanh(first / (jnp.sqrt(second) + 1e-6))
            f_v[ri, j2] = first
            s_v[ri, j2] = second
            k_v[ri, j2] = new
            cols.append(new * sign if ri == 1 else new)
    store_halves(ks, spread_filter(jnp.concatenate(cols, axis=1), consts["order"][...], r))
    exchange(ks, kr, ks_sem, kr_sem)
    stores = [
        pltpu.make_async_copy(k_v, nk_hbm, out_sem.at[0]),
        pltpu.make_async_copy(f_v, nf_hbm, out_sem.at[1]),
        pltpu.make_async_copy(s_v, ns_hbm, out_sem.at[2]),
    ]
    for copy in stores:
        copy.start()
    pltpu.make_async_copy(kr, kr, kr_sem).wait()
    kc[...] = dot(consts["spread_t"][...], halves(kr))

    def inverse_block(d, first):
        q = lax.rem(mb + d, B)
        ys[q] = inverse(
            spec[q], kc[:ROWS], kc[ROWS:], consts["io"][...], consts["tw"][0], consts["tw"][1],
            consts["wh"][...], consts["wl"][...],
        )

        def one(e, carry):
            there = lax.rem(me + e, S)
            pltpu.make_async_remote_copy(
                src_ref=ys.at[q, there],
                dst_ref=yr.at[mb, me],
                send_sem=ys_sem.at[d],
                recv_sem=yr_sem.at[mb],
                device_id={"seq": there, "batch": q},
                device_id_type=pl.DeviceIdType.MESH,
            ).start()
            return carry

        lax.fori_loop(first, S, one, 0)

    inverse_block(0, 1)
    pltpu.make_async_copy(ys.at[mb, me], yr.at[mb, me], yr_sem.at[mb]).start()

    def inverse_step(d, carry):
        inverse_block(d, 0)
        return carry

    lax.fori_loop(1, B, inverse_step, 0)

    def finish_step(d, carry):
        came = lax.rem(mb + B - d, B)
        pltpu.make_async_copy(yr.at[came], yr.at[came], yr_sem.at[came]).wait()
        rows = yr[came].astype(F32).reshape(S * 8, LANES).astype(BF)
        o = unpack_block(rows, consts["unpack"][...])
        at = pl.ds(pl.multiple_of(came * LANES, LANES), LANES)
        y_v[:LANES, at] = o[:, :LANES]
        y_v[LANES:, at] = o[:, LANES:]
        pltpu.make_async_copy(y_v.at[:, at], y_hbm.at[:, at], out_sem.at[3]).start()
        return carry

    lax.fori_loop(0, B, finish_step, 0)

    def drain(d, carry):
        pltpu.make_async_copy(xs.at[0], xs.at[0], xs_sem.at[d]).wait()
        pltpu.make_async_copy(ys.at[0], ys.at[0], ys_sem.at[d]).wait()
        return carry

    for buffer, sem in ((xs.at[0], xs_sem.at[0]), (gs, gs_sem), (ks, ks_sem), (ys.at[0], ys_sem.at[0])):
        part = buffer.at[pl.ds(0, S - 1)]
        pltpu.make_async_copy(part, part, sem).wait()
    lax.fori_loop(1, B, drain, 0)
    for copy in stores:
        copy.wait()
    pltpu.make_async_copy(y_v, y_hbm, out_sem.at[3]).wait()


def hand_over(*refs):
    sems = refs[8]
    copies = [pltpu.make_async_copy(refs[i], refs[4 + i], sems.at[i]) for i in range(4)]
    for copy in copies:
        copy.start()
    for copy in copies:
        copy.wait()


def per_device(inputs, grad_out, spectrum, first_moment, second_moment):
    any_spec = pl.BlockSpec(memory_space=pl.ANY)
    hbm_spec = pl.BlockSpec(memory_space=pltpu.HBM)
    state = (2, 2, C, LANES)
    wide = (C, B * LANES)
    dma = pltpu.SemaphoreType.DMA
    scratch = [pltpu.VMEM(shape, dtype) for shape, dtype in CONSTANTS.values()]
    scratch += [
        pltpu.VMEM(wide, BF),
        pltpu.VMEM(wide, BF),
        pltpu.VMEM(state, F32),
        pltpu.VMEM(state, F32),
        pltpu.VMEM(state, F32),
        pltpu.VMEM(wide, BF),
        pltpu.VMEM((B, S, 16, LANES), BF),
        pltpu.VMEM((B, S, 16, LANES), BF),
        pltpu.VMEM((B, ROWS, 2 * C), F32),
        pltpu.VMEM((ROWS, 2 * C), F32),
        pltpu.VMEM((S, 2, 16, LANES), BF),
        pltpu.VMEM((S, 2, 16, LANES), BF),
        pltpu.VMEM((S, 2, 16, LANES), BF),
        pltpu.VMEM((S, 2, 16, LANES), BF),
        pltpu.VMEM((2 * ROWS, C), F32),
        pltpu.VMEM((B, S, 8, LANES), BF),
        pltpu.VMEM((B, S, 8, LANES), BF),
        pltpu.SemaphoreType.REGULAR((B,)),
        dma((2,)),
        dma((3,)),
        dma((4,)),
        dma((B,)),
        dma((B,)),
        dma,
        dma,
        dma,
        dma,
        dma((B,)),
        dma((B,)),
    ]
    results = pl.pallas_call(
        kernel,
        out_shape=(
            jax.ShapeDtypeStruct(state, F32),
            jax.ShapeDtypeStruct(state, F32),
            jax.ShapeDtypeStruct(state, F32),
            jax.ShapeDtypeStruct(wide, BF),
        ),
        in_specs=[hbm_spec] * 5,
        out_specs=(any_spec,) * 4,
        scratch_shapes=scratch,
        compiler_params=pltpu.CompilerParams(
            collective_id=0, has_side_effects=True, vmem_limit_bytes=48 * 1024 * 1024
        ),
        name="long_convolution_update",
    )(*[pltpu.with_memory_space_constraint(x, pltpu.HBM) for x in (inputs[0], grad_out[0], spectrum, first_moment, second_moment)])
    nk, nf, ns, y = pl.pallas_call(
        hand_over,
        out_shape=[jax.ShapeDtypeStruct(x.shape, x.dtype) for x in results],
        in_specs=[any_spec] * 4,
        out_specs=[hbm_spec] * 4,
        scratch_shapes=[dma((4,))],
        compiler_params=pltpu.CompilerParams(vmem_limit_bytes=1024 * 1024),
        name="hand_over",
    )(*results)
    return nk, nf, ns, y[None]


def solution(mesh):
    state = P(None, "seq", None, "batch")
    rows = P("batch", "seq", None)
    return jax.shard_map(
        per_device,
        mesh=mesh,
        in_specs=(rows, rows, state, state, state),
        out_specs=(state, state, state, rows),
        check_vma=False,
    )
```

```python
import math

import jax
import jax.numpy as jnp
from jax import lax
from jax.experimental import pallas as pl
from jax.experimental.pallas import tpu as pltpu
from jax.sharding import PartitionSpec as P

S = 32
B = 8
C = 256
N = 2 * S * C
LANES = 128
HALF = LANES // 2
K2 = HALF // S
SLOTS = 40
ROWS = K2 * SLOTS
EARLY = 4
BF, F32 = jnp.bfloat16, jnp.float32


def iota(shape, dim):
    return lax.broadcasted_iota(jnp.int32, shape, dim)


def selection(rows, cols, target, transposed=False):
    if transposed:
        return jnp.where(iota((cols, rows), 0) == target(iota((1, rows), 1)), 1.0, 0.0).astype(BF)
    return jnp.where(iota((rows, cols), 1) == target(iota((rows, 1), 0)), 1.0, 0.0).astype(BF)


def pack_at(row):
    p, s, th, k = row >> 8, (row >> 3) & 31, (row >> 1) & 3, row & 1
    return th * LANES + HALF * p + K2 * s + k


def spread_at(row):
    s, ri, j2, k = row >> 3, (row >> 2) & 1, (row >> 1) & 1, row & 1
    j = 2 * s + j2
    return ri * ROWS + k * SLOTS + jnp.where(s < S // 2, j, 2 * S - j)


def order_at(row):
    s, rj, k = row >> 3, (row >> 1) & 3, row & 1
    return rj * HALF + K2 * s + k


def unpack_at(row):
    s, p, h, k = row >> 3, (row >> 2) & 1, (row >> 1) & 1, row & 1
    return h * LANES + HALF * p + K2 * s + k


def make_forward_outer():
    slot = iota((SLOTS, S), 0)
    used = jnp.where(slot <= S, 1.0, 0.0)
    angle = ((slot * iota((SLOTS, S), 1)) & (2 * S - 1)).astype(F32) * (math.pi / S)
    high, low = split(jnp.concatenate([jnp.cos(angle) * used, -jnp.sin(angle) * used], axis=0))
    return jnp.concatenate([high, low], axis=1)


def make_inverse_outer():
    slot = iota((S, SLOTS), 1)
    used = jnp.where(slot <= S, 1.0 / N, 0.0)
    angle = ((slot * iota((S, SLOTS), 0)) & (2 * S - 1)).astype(F32) * (math.pi / S)
    high, low = split(jnp.concatenate([jnp.cos(angle) * used, -jnp.sin(angle) * used], axis=1))
    return jnp.concatenate([high, low, high], axis=1)


def make_twist(ref):
    angle = (iota((SLOTS, C), 0) * iota((SLOTS, C), 1)).astype(F32) * (2 * math.pi / N)
    ref[0] = jnp.cos(angle)
    ref[1] = jnp.sin(angle)


def make_inner(high_ref, low_ref):
    angle = ((iota((C, C), 0) * iota((C, C), 1)) & (C - 1)).astype(F32) * (2 * math.pi / C)
    for x, places in ((jnp.cos(angle), ((0, 0, 1), (1, 1, 1))), (jnp.sin(angle), ((1, 0, 1), (0, 1, -1)))):
        high, low = split(x)
        for i, j, sign in places:
            at = (pl.ds(C * i, C), pl.ds(C * j, C))
            high_ref[at] = high if sign > 0 else -high
            low_ref[at] = low if sign > 0 else -low


CONSTANTS = dict(
    pack=((512, 512), BF),
    fo=((2 * SLOTS, 2 * S), BF),
    wh=((2 * C, 2 * C), BF),
    wl=((2 * C, 2 * C), BF),
    tw=((2, SLOTS, C), F32),
    spread=((256, 2 * ROWS), BF),
    order_t=((256, 256), BF),
    order=((256, 256), BF),
    spread_t=((2 * ROWS, 256), BF),
    io=((S, 6 * SLOTS), BF),
    unpack=((256, 256), BF),
)


def dot(x, y):
    return lax.dot_general(x, y, (((1,), (0,)), ((), ())), preferred_element_type=F32)


def dot_t(x, y):
    return lax.dot_general(x, y, (((1,), (1,)), ((), ())), preferred_element_type=F32)


def split(x):
    high = x.astype(BF)
    return high, (x - high.astype(F32)).astype(BF)


def pack_block(x, g, pack):
    cols = jnp.concatenate([x[:LANES], x[LANES:], g[:LANES], g[LANES:]], axis=1)
    return dot_t(pack, cols).reshape(S, 8, LANES).astype(BF)


def forward(d, fo, tc, ts, wh, wl):
    dt = jnp.swapaxes(d, 0, 1).astype(BF)
    cols = [dt[8 * q + 4 * t + 2 * h + k] for t in range(2) for q in range(2) for k in range(K2) for h in range(2)]
    dc = jnp.concatenate(cols, axis=1)
    z = dot(fo, jnp.concatenate([dc, dc], axis=0))
    re, im = [], []
    for i in range(4 * K2):
        zr = z[:SLOTS, C * i : C * i + C]
        zi = z[SLOTS:, C * i : C * i + C]
        re.append(zr * tc + zi * ts)
        im.append(zi * tc - zr * ts)
    rows = jnp.concatenate([jnp.concatenate(re, axis=0), jnp.concatenate(im, axis=0)], axis=1)
    high, low = split(rows)
    out = dot(high, wh) + dot(low, wh) + dot(high, wl)
    return out[: 2 * ROWS], out[2 * ROWS :]


def product(x, g):
    xr, xi, gr, gi = x[:, :C], x[:, C:], g[:, :C], g[:, C:]
    both = jnp.concatenate([xr * gr + xi * gi, xr * gi - xi * gr], axis=1)
    return both[:ROWS] + both[ROWS:]


def spread_grad(total, spread):
    cols = jnp.concatenate([total[:, :C], total[:, C:]], axis=0) * (1.0 / N)
    return dot(spread, cols.astype(BF))


def turn(flip):
    row = lax.broadcasted_iota(jnp.int32, (C, C), 0)
    col = lax.broadcasted_iota(jnp.int32, (C, C), 1)
    return jnp.where(col == jnp.where(flip, C - 1 - row, row), 1.0, 0.0).astype(BF)


def own_grad(cols, order_t, r):
    return dot_t(r, dot(order_t, cols).astype(BF))


def spread_filter(k, order, r):
    return dot_t(order, dot(r, k.astype(BF)).astype(BF))


def inverse(x, kr, ki, io, tc, ts, wh, wl):
    xr, xi = x[:, :C], x[:, C:]
    kr, ki = jnp.concatenate([kr, kr], axis=0), jnp.concatenate([ki, ki], axis=0)
    high, low = split(jnp.concatenate([xr * kr - xi * ki, xr * ki + xi * kr], axis=1))
    o = dot_t(high, wh) + dot_t(low, wh) + dot_t(high, wl)
    cols = []
    for i in range(2 * K2):
        zr = o[SLOTS * i : SLOTS * (i + 1), :C]
        zi = o[SLOTS * i : SLOTS * (i + 1), C:]
        cols.append(jnp.concatenate([zr * tc - zi * ts, zr * ts + zi * tc], axis=0))
    vh, vl = split(jnp.concatenate(cols, axis=1))
    y = dot(io, jnp.concatenate([vh, vh, vl], axis=0))
    parts = [
        y[:, C * (K2 * q + k) + LANES * h : C * (K2 * q + k) + LANES * (h + 1)]
        for q in range(2)
        for h in range(2)
        for k in range(K2)
    ]
    return jnp.swapaxes(jnp.stack(parts, axis=0), 0, 1)


def unpack_block(y, unpack):
    row = lax.broadcasted_iota(jnp.int32, (LANES, LANES), 0)
    col = lax.broadcasted_iota(jnp.int32, (LANES, LANES), 1)
    eye = jnp.where(row == col, 1.0, 0.0).astype(BF)
    return dot(dot_t(eye, y).astype(BF), unpack).astype(BF)


def cross(x0, x1):
    first = lax.broadcasted_iota(jnp.int32, x0.shape, 1) < HALF
    return (
        jnp.where(first, x0, pltpu.roll(x1, HALF, axis=1)),
        jnp.where(first, pltpu.roll(x0, HALF, axis=1), x1),
    )


def kernel(
    x_hbm, g_hbm, k_hbm, f_hbm, s_hbm, *rest
):
    nk_hbm, nf_hbm, ns_hbm, y_hbm = rest[:4]
    rest = rest[4:]
    consts = dict(zip(CONSTANTS, rest[: len(CONSTANTS)]))
    (
        x_v, g_v, k_v, f_v, s_v, y_v,
        packed, xs, xr, spec, total, gs, gr, ks, kr, kc, ys, yr,
        group_sem, in_sem, state_sem, out_sem,
        xs_sem, xr_sem, gs_sem, gr_sem, ks_sem, kr_sem, ys_sem, yr_sem,
    ) = rest[len(CONSTANTS) :]
    me = lax.axis_index("seq")
    mb = lax.axis_index("batch")

    barrier = pltpu.get_barrier_semaphore()

    def greet_seq(e, carry):
        pl.semaphore_signal(
            barrier, inc=1, device_id={"seq": lax.rem(me + e, S), "batch": mb}, device_id_type=pl.DeviceIdType.MESH
        )
        return carry

    def greet_batch(d, carry):
        pl.semaphore_signal(
            barrier, inc=1, device_id={"seq": me, "batch": lax.rem(mb + d, B)}, device_id_type=pl.DeviceIdType.MESH
        )
        return carry

    def greet_groups(d, carry):
        pl.semaphore_signal(
            group_sem.at[mb],
            inc=1,
            device_id={"seq": me, "batch": lax.rem(mb + d, B)},
            device_id_type=pl.DeviceIdType.MESH,
        )
        return carry

    lax.fori_loop(1, S, greet_seq, 0)
    lax.fori_loop(1, B, greet_batch, 0)

    loads = [
        pltpu.make_async_copy(x_hbm, x_v, in_sem.at[0]),
        pltpu.make_async_copy(g_hbm, g_v, in_sem.at[1]),
    ]
    state_loads = [
        pltpu.make_async_copy(k_hbm, k_v, state_sem.at[0]),
        pltpu.make_async_copy(f_hbm, f_v, state_sem.at[1]),
        pltpu.make_async_copy(s_hbm, s_v, state_sem.at[2]),
    ]
    for copy in loads + state_loads:
        copy.start()
    consts["pack"][...] = selection(512, 512, pack_at)
    for copy in loads:
        copy.wait()

    pl.semaphore_wait(barrier, S - 1 + B - 1)
    lax.fori_loop(1, B, greet_groups, 0)

    def send_block(p, d, first):
        to = lax.rem(mb + d, B)
        cols = pl.ds(pl.multiple_of(to * LANES, LANES), LANES)
        rows = pl.ds(256 * p, 256)
        xs[p, to] = pack_block(x_v[:, cols], g_v[:, cols], consts["pack"][rows])
        if p == 0 and first == 0:
            pl.semaphore_wait(group_sem.at[to], 1)

        def one(e, carry):
            there = lax.rem(me + e, S)
            pltpu.make_async_remote_copy(
                src_ref=xs.at[p, to, there],
                dst_ref=xr.at[p, mb, me],
                send_sem=xs_sem.at[p, d],
                recv_sem=xr_sem.at[p, mb],
                device_id={"seq": there, "batch": to},
                device_id_type=pl.DeviceIdType.MESH,
            ).start()
            return carry

        lax.fori_loop(first, S, one, 0)

    def send_own(p):
        send_block(p, 0, 1)
        pltpu.make_async_copy(xs.at[p, mb, me], xr.at[p, mb, me], xr_sem.at[p, mb]).start()

    def send_blocks(p, start, stop):
        def step(d, carry):
            send_block(p, d, 0)
            return carry

        lax.fori_loop(start, stop, step, 0)

    send_own(0)
    send_blocks(0, 1, B)
    send_own(1)
    send_blocks(1, 1, EARLY)
    consts["fo"][...] = make_forward_outer()
    make_twist(consts["tw"])
    make_inner(consts["wh"], consts["wl"])
    consts["spread"][...] = selection(256, 2 * ROWS, spread_at)
    consts["spread_t"][...] = selection(256, 2 * ROWS, spread_at, True)
    consts["order"][...] = selection(256, 256, order_at)
    consts["order_t"][...] = selection(256, 256, order_at, True)
    consts["io"][...] = make_inverse_outer()
    consts["unpack"][...] = selection(256, 256, unpack_at)
    for copy in state_loads:
        copy.wait()
    for i, ref in enumerate((k_v, f_v, s_v)):
        for ri in range(2):
            packed[i, 0, ri], packed[i, 1, ri] = cross(ref[ri, 0], ref[ri, 1])
    total[...] = jnp.zeros_like(total)

    def pair(i):
        return [lax.rem(mb + B - 2 * i - q, B) for q in range(2)]

    def forward_pair(p, i):
        for q in pair(i):
            pltpu.make_async_copy(xr.at[p, q], xr.at[p, q], xr_sem.at[p, q]).wait()
        sx, sg = forward(
            jnp.concatenate([xr[p, q].astype(F32) for q in pair(i)], axis=1),
            consts["fo"][...],
            consts["tw"][0],
            consts["tw"][1],
            consts["wh"][...],
            consts["wl"][...],
        )
        spec[p, i] = sx
        total[p] += product(sx, sg)

    def forward_pairs(p, start, stop):
        def step(i, carry):
            forward_pair(p, i)
            return carry

        lax.fori_loop(start, stop, step, 0)

    def exchange(sent, landed, send_sem, recv_sem):
        pltpu.make_async_copy(sent.at[me], landed.at[me], recv_sem).start()

        def one(e, carry):
            there = lax.rem(me + e, S)
            pltpu.make_async_remote_copy(
                src_ref=sent.at[there],
                dst_ref=landed.at[me],
                send_sem=send_sem,
                recv_sem=recv_sem,
                device_id={"seq": there, "batch": mb},
                device_id_type=pl.DeviceIdType.MESH,
            ).start()
            return carry

        lax.fori_loop(1, S, one, 0)

    def store_halves(ref, value):
        for h in range(2):
            ref[:, h] = value[:, LANES * h : LANES * (h + 1)].reshape(S, 8, LANES).astype(BF)

    def halves(ref):
        return jnp.concatenate(
            [ref[:, h].astype(F32).reshape(S * 8, LANES).astype(BF) for h in range(2)], axis=1
        )

    def send_grad(p):
        store_halves(gs.at[p], spread_grad(total[p], consts["spread"][...]))
        exchange(gs.at[p], gr.at[p], gs_sem.at[p], gr_sem.at[p])

    flip = me >= S // 2
    sign = jnp.where(flip, -1.0, 1.0).astype(F32)

    def update(p):
        r = turn(flip)
        pltpu.make_async_copy(gr.at[p], gr.at[p], gr_sem.at[p]).wait()
        grad = own_grad(halves(gr.at[p]), consts["order_t"][...], r)
        cols = []
        for ri in range(2):
            part = grad[:, LANES * ri : LANES * (ri + 1)]
            if ri == 1:
                part = part * sign
            first = 0.9 * packed[1, p, ri] + 0.1 * part
            second = 0.99 * packed[2, p, ri] + 0.01 * part * part
            new = packed[0, p, ri] - 0.5 * jnp.tanh(first / (jnp.sqrt(second) + 1e-6))
            packed[0, p, ri] = new
            packed[1, p, ri] = first
            packed[2, p, ri] = second
            cols.append(new * sign if ri == 1 else new)
        store_halves(ks.at[p], spread_filter(jnp.concatenate(cols, axis=1), consts["order"][...], r))
        exchange(ks.at[p], kr.at[p], ks_sem.at[p], kr_sem.at[p])

    def inverse_pair(p, i, own):
        y = inverse(
            spec[p, i], kc[p, :ROWS], kc[p, ROWS:], consts["io"][...], consts["tw"][0], consts["tw"][1],
            consts["wh"][...], consts["wl"][...],
        )
        for part, q in enumerate(pair(i)):
            ys[p, q] = y[:, 4 * part : 4 * part + 4].astype(BF)

            def one(e, carry):
                there = lax.rem(me + e, S)
                pltpu.make_async_remote_copy(
                    src_ref=ys.at[p, q, there],
                    dst_ref=yr.at[p, mb, me],
                    send_sem=ys_sem.at[p, q],
                    recv_sem=yr_sem.at[p, mb],
                    device_id={"seq": there, "batch": q},
                    device_id_type=pl.DeviceIdType.MESH,
                ).start()
                return carry

            lax.fori_loop(1 if own and part == 0 else 0, S, one, 0)

    def inverse_half(p):
        pltpu.make_async_copy(kr.at[p], kr.at[p], kr_sem.at[p]).wait()
        kc[p] = dot(consts["spread_t"][...], halves(kr.at[p]))
        inverse_pair(p, 0, True)
        pltpu.make_async_copy(ys.at[p, mb, me], yr.at[p, mb, me], yr_sem.at[p, mb]).start()

        def step(i, carry):
            inverse_pair(p, i, False)
            return carry

        lax.fori_loop(1, B // 2, step, 0)

    forward_pairs(0, 0, 4)
    send_grad(0)
    send_blocks(1, EARLY, B)
    forward_pairs(1, 0, 2)
    update(0)
    forward_pairs(1, 2, 4)
    send_grad(1)
    inverse_half(0)
    update(1)
    for i, ref in enumerate((k_v, f_v, s_v)):
        for ri in range(2):
            ref[ri, 0], ref[ri, 1] = cross(packed[i, 0, ri], packed[i, 1, ri])
    stores = [
        pltpu.make_async_copy(k_v, nk_hbm, out_sem.at[0]),
        pltpu.make_async_copy(f_v, nf_hbm, out_sem.at[1]),
        pltpu.make_async_copy(s_v, ns_hbm, out_sem.at[2]),
    ]
    for copy in stores:
        copy.start()
    inverse_half(1)

    def finish_step(d, carry):
        came = lax.rem(mb + d, B)
        for p in range(2):
            pltpu.make_async_copy(yr.at[p, came], yr.at[p, came], yr_sem.at[p, came]).wait()
        rows = jnp.concatenate([yr[p, came].astype(F32) for p in range(2)], axis=1)
        o = unpack_block(rows.reshape(S * 8, LANES).astype(BF), consts["unpack"][...])
        at = pl.ds(pl.multiple_of(came * LANES, LANES), LANES)
        y_v[:LANES, at] = o[:, :LANES]
        y_v[LANES:, at] = o[:, LANES:]
        pltpu.make_async_copy(y_v.at[:, at], y_hbm.at[:, at], out_sem.at[3]).start()
        return carry

    lax.fori_loop(0, B, finish_step, 0)

    for p in range(2):

        def drain(d, carry):
            other = lax.rem(mb + d, B)
            pltpu.make_async_copy(xs.at[p, 0], xs.at[p, 0], xs_sem.at[p, d]).wait()
            pltpu.make_async_copy(ys.at[p, 0], ys.at[p, 0], ys_sem.at[p, other]).wait()
            return carry

        for buffer, sem in (
            (xs.at[p, 0], xs_sem.at[p, 0]),
            (gs.at[p], gs_sem.at[p]),
            (ks.at[p], ks_sem.at[p]),
            (ys.at[p, 0], ys_sem.at[p, mb]),
        ):
            part = buffer.at[pl.ds(0, S - 1)]
            pltpu.make_async_copy(part, part, sem).wait()
        lax.fori_loop(1, B, drain, 0)
    for copy in stores:
        copy.wait()
    pltpu.make_async_copy(y_v, y_hbm, out_sem.at[3]).wait()


def hand_over(*refs):
    sems = refs[8]
    copies = [pltpu.make_async_copy(refs[i], refs[4 + i], sems.at[i]) for i in range(4)]
    for copy in copies:
        copy.start()
    for copy in copies:
        copy.wait()


def per_device(inputs, grad_out, spectrum, first_moment, second_moment):
    any_spec = pl.BlockSpec(memory_space=pl.ANY)
    hbm_spec = pl.BlockSpec(memory_space=pltpu.HBM)
    state = (2, 2, C, LANES)
    wide = (C, B * LANES)
    dma = pltpu.SemaphoreType.DMA
    scratch = [pltpu.VMEM(shape, dtype) for shape, dtype in CONSTANTS.values()]
    scratch += [
        pltpu.VMEM(wide, BF),
        pltpu.VMEM(wide, BF),
        pltpu.VMEM(state, F32),
        pltpu.VMEM(state, F32),
        pltpu.VMEM(state, F32),
        pltpu.VMEM(wide, BF),
        pltpu.VMEM((3, 2, 2, C, LANES), F32),
        pltpu.VMEM((2, B, S, 8, LANES), BF),
        pltpu.VMEM((2, B, S, 8, LANES), BF),
        pltpu.VMEM((2, B // 2, 2 * ROWS, 2 * C), F32),
        pltpu.VMEM((2, ROWS, 2 * C), F32),
        pltpu.VMEM((2, S, 2, 8, LANES), BF),
        pltpu.VMEM((2, S, 2, 8, LANES), BF),
        pltpu.VMEM((2, S, 2, 8, LANES), BF),
        pltpu.VMEM((2, S, 2, 8, LANES), BF),
        pltpu.VMEM((2, 2 * ROWS, C), F32),
        pltpu.VMEM((2, B, S, 4, LANES), BF),
        pltpu.VMEM((2, B, S, 4, LANES), BF),
        pltpu.SemaphoreType.REGULAR((B,)),
        dma((2,)),
        dma((3,)),
        dma((4,)),
        dma((2, B)),
        dma((2, B)),
        dma((2,)),
        dma((2,)),
        dma((2,)),
        dma((2,)),
        dma((2, B)),
        dma((2, B)),
    ]
    results = pl.pallas_call(
        kernel,
        out_shape=(
            jax.ShapeDtypeStruct(state, F32),
            jax.ShapeDtypeStruct(state, F32),
            jax.ShapeDtypeStruct(state, F32),
            jax.ShapeDtypeStruct(wide, BF),
        ),
        in_specs=[hbm_spec] * 5,
        out_specs=(any_spec,) * 4,
        scratch_shapes=scratch,
        compiler_params=pltpu.CompilerParams(
            collective_id=0, has_side_effects=True, vmem_limit_bytes=48 * 1024 * 1024
        ),
        name="long_convolution_update",
    )(*[pltpu.with_memory_space_constraint(x, pltpu.HBM) for x in (inputs[0], grad_out[0], spectrum, first_moment, second_moment)])
    nk, nf, ns, y = pl.pallas_call(
        hand_over,
        out_shape=[jax.ShapeDtypeStruct(x.shape, x.dtype) for x in results],
        in_specs=[any_spec] * 4,
        out_specs=[hbm_spec] * 4,
        scratch_shapes=[dma((4,))],
        compiler_params=pltpu.CompilerParams(vmem_limit_bytes=1024 * 1024),
        name="hand_over",
    )(*results)
    return nk, nf, ns, y[None]


def solution(mesh):
    state = P(None, "seq", None, "batch")
    rows = P("batch", "seq", None)
    return jax.shard_map(
        per_device,
        mesh=mesh,
        in_specs=(rows, rows, state, state, state),
        out_specs=(state, state, state, rows),
        check_vma=False,
    )
```

```python
import math

import jax
import jax.numpy as jnp
from jax import lax
from jax.experimental import pallas as pl
from jax.experimental.pallas import tpu as pltpu
from jax.sharding import PartitionSpec as P

S = 32
B = 8
C = 256
N = 2 * S * C
LANES = 128
HALF = LANES // 2
K2 = HALF // S
SLOTS = 40
ROWS = K2 * SLOTS
BF, F32 = jnp.bfloat16, jnp.float32


def iota(shape, dim):
    return lax.broadcasted_iota(jnp.int32, shape, dim)


def selection(rows, cols, target, transposed=False):
    if transposed:
        return jnp.where(iota((cols, rows), 0) == target(iota((1, rows), 1)), 1.0, 0.0).astype(BF)
    return jnp.where(iota((rows, cols), 1) == target(iota((rows, 1), 0)), 1.0, 0.0).astype(BF)


def pack_at(row):
    p, s, th, k = row >> 8, (row >> 3) & 31, (row >> 1) & 3, row & 1
    return th * LANES + HALF * p + K2 * s + k


def spread_at(row):
    s, ri, j2, k = row >> 3, (row >> 2) & 1, (row >> 1) & 1, row & 1
    j = 2 * s + j2
    return ri * ROWS + k * SLOTS + jnp.where(s < S // 2, j, 2 * S - j)


def order_at(row):
    s, rj, k = row >> 3, (row >> 1) & 3, row & 1
    return rj * HALF + K2 * s + k


def unpack_at(row):
    s, p, h, k = row >> 3, (row >> 2) & 1, (row >> 1) & 1, row & 1
    return h * LANES + HALF * p + K2 * s + k


def make_forward_outer():
    slot = iota((SLOTS, S), 0)
    used = jnp.where(slot <= S, 1.0, 0.0)
    angle = ((slot * iota((SLOTS, S), 1)) & (2 * S - 1)).astype(F32) * (math.pi / S)
    high, low = split(jnp.concatenate([jnp.cos(angle) * used, -jnp.sin(angle) * used], axis=0))
    return jnp.concatenate([high, low], axis=1)


def make_inverse_outer():
    slot = iota((S, SLOTS), 1)
    used = jnp.where(slot <= S, 1.0 / N, 0.0)
    angle = ((slot * iota((S, SLOTS), 0)) & (2 * S - 1)).astype(F32) * (math.pi / S)
    high, low = split(jnp.concatenate([jnp.cos(angle) * used, -jnp.sin(angle) * used], axis=1))
    return jnp.concatenate([high, low, high], axis=1)


def make_twist(ref):
    angle = (iota((SLOTS, C), 0) * iota((SLOTS, C), 1)).astype(F32) * (2 * math.pi / N)
    ref[0] = jnp.cos(angle)
    ref[1] = jnp.sin(angle)


def make_inner(high_ref, low_ref):
    angle = ((iota((C, C), 0) * iota((C, C), 1)) & (C - 1)).astype(F32) * (2 * math.pi / C)
    for x, places in ((jnp.cos(angle), ((0, 0, 1), (1, 1, 1))), (jnp.sin(angle), ((1, 0, 1), (0, 1, -1)))):
        high, low = split(x)
        for i, j, sign in places:
            at = (pl.ds(C * i, C), pl.ds(C * j, C))
            high_ref[at] = high if sign > 0 else -high
            low_ref[at] = low if sign > 0 else -low


CONSTANTS = dict(
    pack=((512, 512), BF),
    fo=((2 * SLOTS, 2 * S), BF),
    wh=((2 * C, 2 * C), BF),
    wl=((2 * C, 2 * C), BF),
    tw=((2, SLOTS, C), F32),
    spread=((256, 2 * ROWS), BF),
    order_t=((256, 256), BF),
    order=((256, 256), BF),
    spread_t=((2 * ROWS, 256), BF),
    io=((S, 6 * SLOTS), BF),
    unpack=((256, 256), BF),
)


def dot(x, y):
    return lax.dot_general(x, y, (((1,), (0,)), ((), ())), preferred_element_type=F32)


def dot_t(x, y):
    return lax.dot_general(x, y, (((1,), (1,)), ((), ())), preferred_element_type=F32)


def split(x):
    high = x.astype(BF)
    return high, (x - high.astype(F32)).astype(BF)


def pack_block(x, g, pack):
    cols = jnp.concatenate([x[:LANES], x[LANES:], g[:LANES], g[LANES:]], axis=1)
    return dot_t(pack, cols).reshape(S, 8, LANES).astype(BF)


def forward(d, fo, tc, ts, wh, wl):
    dt = jnp.swapaxes(d, 0, 1).astype(BF)
    cols = [dt[8 * q + 4 * t + 2 * h + k] for t in range(2) for q in range(2) for k in range(K2) for h in range(2)]
    dc = jnp.concatenate(cols, axis=1)
    z = dot(fo, jnp.concatenate([dc, dc], axis=0))
    re, im = [], []
    for i in range(4 * K2):
        zr = z[:SLOTS, C * i : C * i + C]
        zi = z[SLOTS:, C * i : C * i + C]
        re.append(zr * tc + zi * ts)
        im.append(zi * tc - zr * ts)
    rows = jnp.concatenate([jnp.concatenate(re, axis=0), jnp.concatenate(im, axis=0)], axis=1)
    high, low = split(rows)
    out = dot(high, wh) + dot(low, wh) + dot(high, wl)
    return out[: 2 * ROWS], out[2 * ROWS :]


def product(x, g):
    xr, xi, gr, gi = x[:, :C], x[:, C:], g[:, :C], g[:, C:]
    both = jnp.concatenate([xr * gr + xi * gi, xr * gi - xi * gr], axis=1)
    return both[:ROWS] + both[ROWS:]


def spread_grad(total, spread):
    cols = jnp.concatenate([total[:, :C], total[:, C:]], axis=0) * (1.0 / N)
    return dot(spread, cols.astype(BF))


def turn(flip):
    row = lax.broadcasted_iota(jnp.int32, (C, C), 0)
    col = lax.broadcasted_iota(jnp.int32, (C, C), 1)
    return jnp.where(col == jnp.where(flip, C - 1 - row, row), 1.0, 0.0).astype(BF)


def own_grad(cols, order_t, r):
    return dot_t(r, dot(order_t, cols).astype(BF))


def spread_filter(k, order, r):
    return dot_t(order, dot(r, k.astype(BF)).astype(BF))


def inverse(x, kr, ki, io, tc, ts, wh, wl):
    xr, xi = x[:, :C], x[:, C:]
    kr, ki = jnp.concatenate([kr, kr], axis=0), jnp.concatenate([ki, ki], axis=0)
    mixed = jnp.concatenate([xr * kr - xi * ki, xr * ki + xi * kr], axis=1).astype(BF)
    o = dot_t(mixed, wh) + dot_t(mixed, wl)
    cols = []
    for i in range(2 * K2):
        zr = o[SLOTS * i : SLOTS * (i + 1), :C]
        zi = o[SLOTS * i : SLOTS * (i + 1), C:]
        cols.append(jnp.concatenate([zr * tc - zi * ts, zr * ts + zi * tc], axis=0))
    vh, vl = split(jnp.concatenate(cols, axis=1))
    y = dot(io, jnp.concatenate([vh, vh, vl], axis=0))
    parts = [
        y[:, C * (K2 * q + k) + LANES * h : C * (K2 * q + k) + LANES * (h + 1)]
        for q in range(2)
        for h in range(2)
        for k in range(K2)
    ]
    return jnp.swapaxes(jnp.stack(parts, axis=0), 0, 1)


def unpack_block(y, unpack):
    row = lax.broadcasted_iota(jnp.int32, (LANES, LANES), 0)
    col = lax.broadcasted_iota(jnp.int32, (LANES, LANES), 1)
    eye = jnp.where(row == col, 1.0, 0.0).astype(BF)
    return dot(dot_t(eye, y).astype(BF), unpack).astype(BF)


def cross(x0, x1):
    first = lax.broadcasted_iota(jnp.int32, x0.shape, 1) < HALF
    return (
        jnp.where(first, x0, pltpu.roll(x1, HALF, axis=1)),
        jnp.where(first, pltpu.roll(x0, HALF, axis=1), x1),
    )


def kernel(
    x_hbm, g_hbm, k_hbm, f_hbm, s_hbm, *rest
):
    nk_hbm, nf_hbm, ns_hbm, y_hbm = rest[:4]
    rest = rest[4:]
    consts = dict(zip(CONSTANTS, rest[: len(CONSTANTS)]))
    (
        x_v, g_v, k_v, f_v, s_v, y_v,
        packed, xs, xr, spec, total, gs, gr, ks, kr, kc, ys, yr,
        group_sem, in_sem, state_sem, out_sem,
        xs_sem, xr_sem, gs_sem, gr_sem, ks_sem, kr_sem, ys_sem, yr_sem,
    ) = rest[len(CONSTANTS) :]
    me = lax.axis_index("seq")
    mb = lax.axis_index("batch")

    barrier = pltpu.get_barrier_semaphore()

    def greet_seq(e, carry):
        pl.semaphore_signal(
            barrier, inc=1, device_id={"seq": lax.rem(me + e, S), "batch": mb}, device_id_type=pl.DeviceIdType.MESH
        )
        return carry

    def greet_batch(d, carry):
        pl.semaphore_signal(
            barrier, inc=1, device_id={"seq": me, "batch": lax.rem(mb + d, B)}, device_id_type=pl.DeviceIdType.MESH
        )
        return carry

    def greet_groups(d, carry):
        pl.semaphore_signal(
            group_sem.at[mb],
            inc=1,
            device_id={"seq": me, "batch": lax.rem(mb + d, B)},
            device_id_type=pl.DeviceIdType.MESH,
        )
        return carry

    lax.fori_loop(1, S, greet_seq, 0)
    lax.fori_loop(1, B, greet_batch, 0)

    loads = [
        pltpu.make_async_copy(x_hbm, x_v, in_sem.at[0]),
        pltpu.make_async_copy(g_hbm, g_v, in_sem.at[1]),
    ]
    state_loads = [
        pltpu.make_async_copy(k_hbm, k_v, state_sem.at[0]),
        pltpu.make_async_copy(f_hbm, f_v, state_sem.at[1]),
        pltpu.make_async_copy(s_hbm, s_v, state_sem.at[2]),
    ]
    for copy in loads + state_loads:
        copy.start()
    consts["pack"][...] = selection(512, 512, pack_at)
    for copy in loads:
        copy.wait()

    def pack(p, to):
        cols = pl.ds(pl.multiple_of(to * LANES, LANES), LANES)
        rows = pl.ds(256 * p, 256)
        xs[p, to] = pack_block(x_v[:, cols], g_v[:, cols], consts["pack"][rows])

    pack(0, mb)
    pl.semaphore_wait(barrier, S - 1 + B - 1)
    lax.fori_loop(1, B, greet_groups, 0)

    def send_block(p, d, first):
        to = lax.rem(mb + d, B)
        if p == 1 or first == 0:
            pack(p, to)
        if p == 0 and first == 0:
            pl.semaphore_wait(group_sem.at[to], 1)

        def one(e, carry):
            there = lax.rem(me + e, S)
            pltpu.make_async_remote_copy(
                src_ref=xs.at[p, to, there],
                dst_ref=xr.at[p, mb, me],
                send_sem=xs_sem.at[p, d],
                recv_sem=xr_sem.at[p, mb],
                device_id={"seq": there, "batch": to},
                device_id_type=pl.DeviceIdType.MESH,
            ).start()
            return carry

        lax.fori_loop(first, S, one, 0, unroll=8 if first == 0 else 1)

    def send_own(p):
        send_block(p, 0, 1)
        pltpu.make_async_copy(xs.at[p, mb, me], xr.at[p, mb, me], xr_sem.at[p, mb]).start()

    def send_blocks(p, start, stop):
        def step(d, carry):
            send_block(p, d, 0)
            return carry

        lax.fori_loop(start, stop, step, 0)

    send_own(0)
    send_own(1)
    send_blocks(0, 1, B)
    send_blocks(1, 1, B)
    consts["fo"][...] = make_forward_outer()
    make_twist(consts["tw"])
    make_inner(consts["wh"], consts["wl"])
    consts["spread"][...] = selection(256, 2 * ROWS, spread_at)
    consts["spread_t"][...] = selection(256, 2 * ROWS, spread_at, True)
    consts["order"][...] = selection(256, 256, order_at)
    consts["order_t"][...] = selection(256, 256, order_at, True)
    consts["io"][...] = make_inverse_outer()
    consts["unpack"][...] = selection(256, 256, unpack_at)
    for copy in state_loads:
        copy.wait()
    for i, ref in enumerate((k_v, f_v, s_v)):
        for ri in range(2):
            packed[i, 0, ri], packed[i, 1, ri] = cross(ref[ri, 0], ref[ri, 1])
    total[...] = jnp.zeros_like(total)

    def pair(i):
        return [lax.rem(mb + B - 2 * i - q, B) for q in range(2)]

    def forward_pair(p, i):
        for q in pair(i):
            pltpu.make_async_copy(xr.at[p, q], xr.at[p, q], xr_sem.at[p, q]).wait()
        sx, sg = forward(
            jnp.concatenate([xr[p, q].astype(F32) for q in pair(i)], axis=1),
            consts["fo"][...],
            consts["tw"][0],
            consts["tw"][1],
            consts["wh"][...],
            consts["wl"][...],
        )
        spec[p, i] = sx
        total[p] += product(sx, sg)

    def forward_pairs(p, start, stop):
        def step(i, carry):
            forward_pair(p, i)
            return carry

        lax.fori_loop(start, stop, step, 0)

    def exchange(sent, landed, send_sem, recv_sem):
        pltpu.make_async_copy(sent.at[me], landed.at[me], recv_sem).start()

        def one(e, carry):
            there = lax.rem(me + e, S)
            pltpu.make_async_remote_copy(
                src_ref=sent.at[there],
                dst_ref=landed.at[me],
                send_sem=send_sem,
                recv_sem=recv_sem,
                device_id={"seq": there, "batch": mb},
                device_id_type=pl.DeviceIdType.MESH,
            ).start()
            return carry

        lax.fori_loop(1, S, one, 0)

    def store_halves(ref, value):
        for h in range(2):
            ref[:, h] = value[:, LANES * h : LANES * (h + 1)].reshape(S, 8, LANES).astype(BF)

    def halves(ref):
        return jnp.concatenate(
            [ref[:, h].astype(F32).reshape(S * 8, LANES).astype(BF) for h in range(2)], axis=1
        )

    def send_grad(p):
        store_halves(gs.at[p], spread_grad(total[p], consts["spread"][...]))
        exchange(gs.at[p], gr.at[p], gs_sem.at[p], gr_sem.at[p])

    flip = me >= S // 2
    sign = jnp.where(flip, -1.0, 1.0).astype(F32)

    def update(p):
        r = turn(flip)
        pltpu.make_async_copy(gr.at[p], gr.at[p], gr_sem.at[p]).wait()
        grad = own_grad(halves(gr.at[p]), consts["order_t"][...], r)
        cols = []
        for ri in range(2):
            part = grad[:, LANES * ri : LANES * (ri + 1)]
            if ri == 1:
                part = part * sign
            first = 0.9 * packed[1, p, ri] + 0.1 * part
            second = 0.99 * packed[2, p, ri] + 0.01 * part * part
            new = packed[0, p, ri] - 0.5 * jnp.tanh(first / (jnp.sqrt(second) + 1e-6))
            packed[0, p, ri] = new
            packed[1, p, ri] = first
            packed[2, p, ri] = second
            cols.append(new * sign if ri == 1 else new)
        store_halves(ks.at[p], spread_filter(jnp.concatenate(cols, axis=1), consts["order"][...], r))
        exchange(ks.at[p], kr.at[p], ks_sem.at[p], kr_sem.at[p])

    def inverse_pair(p, i, own):
        y = inverse(
            spec[p, i], kc[p, :ROWS], kc[p, ROWS:], consts["io"][...], consts["tw"][0], consts["tw"][1],
            consts["wh"][...], consts["wl"][...],
        )
        for part, q in enumerate(pair(i)):
            ys[p, q] = y[:, 4 * part : 4 * part + 4].astype(BF)

            def one(e, carry):
                there = lax.rem(me + e, S)
                pltpu.make_async_remote_copy(
                    src_ref=ys.at[p, q, there],
                    dst_ref=yr.at[p, mb, me],
                    send_sem=ys_sem.at[p, q],
                    recv_sem=yr_sem.at[p, mb],
                    device_id={"seq": there, "batch": q},
                    device_id_type=pl.DeviceIdType.MESH,
                ).start()
                return carry

            lax.fori_loop(1 if own and part == 0 else 0, S, one, 0, unroll=1 if own and part == 0 else 8)

    def inverse_start(p):
        pltpu.make_async_copy(kr.at[p], kr.at[p], kr_sem.at[p]).wait()
        kc[p] = dot(consts["spread_t"][...], halves(kr.at[p]))
        inverse_pair(p, 0, True)
        pltpu.make_async_copy(ys.at[p, mb, me], yr.at[p, mb, me], yr_sem.at[p, mb]).start()

    def inverse_pairs(p, start, stop):
        def step(i, carry):
            inverse_pair(p, i, False)
            return carry

        lax.fori_loop(start, stop, step, 0)

    forward_pairs(0, 0, 4)
    send_grad(0)
    forward_pairs(1, 0, 4)
    send_grad(1)
    update(0)
    update(1)
    inverse_start(0)
    inverse_pairs(0, 1, B // 2)
    for i, ref in enumerate((k_v, f_v, s_v)):
        for ri in range(2):
            ref[ri, 0], ref[ri, 1] = cross(packed[i, 0, ri], packed[i, 1, ri])
    stores = [
        pltpu.make_async_copy(k_v, nk_hbm, out_sem.at[0]),
        pltpu.make_async_copy(f_v, nf_hbm, out_sem.at[1]),
        pltpu.make_async_copy(s_v, ns_hbm, out_sem.at[2]),
    ]
    for copy in stores:
        copy.start()
    inverse_start(1)
    inverse_pairs(1, 1, B // 2)

    def finish_step(d, carry):
        came = lax.rem(mb + d, B)
        for p in range(2):
            pltpu.make_async_copy(yr.at[p, came], yr.at[p, came], yr_sem.at[p, came]).wait()
        rows = jnp.concatenate([yr[p, came].astype(F32) for p in range(2)], axis=1)
        o = unpack_block(rows.reshape(S * 8, LANES).astype(BF), consts["unpack"][...])
        at = pl.ds(pl.multiple_of(came * LANES, LANES), LANES)
        y_v[:LANES, at] = o[:, :LANES]
        y_v[LANES:, at] = o[:, LANES:]
        pltpu.make_async_copy(y_v.at[:, at], y_hbm.at[:, at], out_sem.at[3]).start()
        return carry

    lax.fori_loop(0, B, finish_step, 0)

    for p in range(2):

        def drain(d, carry):
            other = lax.rem(mb + d, B)
            pltpu.make_async_copy(xs.at[p, 0], xs.at[p, 0], xs_sem.at[p, d]).wait()
            pltpu.make_async_copy(ys.at[p, 0], ys.at[p, 0], ys_sem.at[p, other]).wait()
            return carry

        for buffer, sem in (
            (xs.at[p, 0], xs_sem.at[p, 0]),
            (gs.at[p], gs_sem.at[p]),
            (ks.at[p], ks_sem.at[p]),
            (ys.at[p, 0], ys_sem.at[p, mb]),
        ):
            part = buffer.at[pl.ds(0, S - 1)]
            pltpu.make_async_copy(part, part, sem).wait()
        lax.fori_loop(1, B, drain, 0)
    for copy in stores:
        copy.wait()
    pltpu.make_async_copy(y_v, y_hbm, out_sem.at[3]).wait()


def hand_over(*refs):
    sems = refs[8]
    copies = []
    for i in range(4):
        count = 2 if i < 3 else 4
        size = refs[i].shape[0] // count
        for j in range(count):
            part = pl.ds(j * size, size)
            copies.append(pltpu.make_async_copy(refs[i].at[part], refs[4 + i].at[part], sems.at[i, j]))
    for copy in copies:
        copy.start()
    for copy in copies:
        copy.wait()


def per_device(inputs, grad_out, spectrum, first_moment, second_moment):
    any_spec = pl.BlockSpec(memory_space=pl.ANY)
    hbm_spec = pl.BlockSpec(memory_space=pltpu.HBM)
    state = (2, 2, C, LANES)
    wide = (C, B * LANES)
    dma = pltpu.SemaphoreType.DMA
    scratch = [pltpu.VMEM(shape, dtype) for shape, dtype in CONSTANTS.values()]
    scratch += [
        pltpu.VMEM(wide, BF),
        pltpu.VMEM(wide, BF),
        pltpu.VMEM(state, F32),
        pltpu.VMEM(state, F32),
        pltpu.VMEM(state, F32),
        pltpu.VMEM(wide, BF),
        pltpu.VMEM((3, 2, 2, C, LANES), F32),
        pltpu.VMEM((2, B, S, 8, LANES), BF),
        pltpu.VMEM((2, B, S, 8, LANES), BF),
        pltpu.VMEM((2, B // 2, 2 * ROWS, 2 * C), F32),
        pltpu.VMEM((2, ROWS, 2 * C), F32),
        pltpu.VMEM((2, S, 2, 8, LANES), BF),
        pltpu.VMEM((2, S, 2, 8, LANES), BF),
        pltpu.VMEM((2, S, 2, 8, LANES), BF),
        pltpu.VMEM((2, S, 2, 8, LANES), BF),
        pltpu.VMEM((2, 2 * ROWS, C), F32),
        pltpu.VMEM((2, B, S, 4, LANES), BF),
        pltpu.VMEM((2, B, S, 4, LANES), BF),
        pltpu.SemaphoreType.REGULAR((B,)),
        dma((2,)),
        dma((3,)),
        dma((4,)),
        dma((2, B)),
        dma((2, B)),
        dma((2,)),
        dma((2,)),
        dma((2,)),
        dma((2,)),
        dma((2, B)),
        dma((2, B)),
    ]
    results = pl.pallas_call(
        kernel,
        out_shape=(
            jax.ShapeDtypeStruct(state, F32),
            jax.ShapeDtypeStruct(state, F32),
            jax.ShapeDtypeStruct(state, F32),
            jax.ShapeDtypeStruct(wide, BF),
        ),
        in_specs=[hbm_spec] * 5,
        out_specs=(any_spec,) * 4,
        scratch_shapes=scratch,
        compiler_params=pltpu.CompilerParams(
            collective_id=0, has_side_effects=True, vmem_limit_bytes=48 * 1024 * 1024
        ),
        name="long_convolution_update",
    )(*[pltpu.with_memory_space_constraint(x, pltpu.HBM) for x in (inputs[0], grad_out[0], spectrum, first_moment, second_moment)])
    nk, nf, ns, y = pl.pallas_call(
        hand_over,
        out_shape=[jax.ShapeDtypeStruct(x.shape, x.dtype) for x in results],
        in_specs=[any_spec] * 4,
        out_specs=[hbm_spec] * 4,
        scratch_shapes=[dma((4, 4))],
        compiler_params=pltpu.CompilerParams(vmem_limit_bytes=1024 * 1024),
        name="hand_over",
    )(*results)
    return nk, nf, ns, y[None]


def solution(mesh):
    state = P(None, "seq", None, "batch")
    rows = P("batch", "seq", None)
    return jax.shard_map(
        per_device,
        mesh=mesh,
        in_specs=(rows, rows, state, state, state),
        out_specs=(state, state, state, rows),
        check_vma=False,
    )
```

```python
import math

import jax
import jax.numpy as jnp
from jax import lax
from jax.experimental import pallas as pl
from jax.experimental.pallas import tpu as pltpu
from jax.sharding import PartitionSpec as P

S = 32
B = 8
C = 256
N = 2 * S * C
LANES = 128
HALF = LANES // 2
K2 = HALF // S
SLOTS = 40
ROWS = K2 * SLOTS
BF, F32 = jnp.bfloat16, jnp.float32


def iota(shape, dim):
    return lax.broadcasted_iota(jnp.int32, shape, dim)


def selection(rows, cols, target, transposed=False):
    if transposed:
        return jnp.where(iota((cols, rows), 0) == target(iota((1, rows), 1)), 1.0, 0.0).astype(BF)
    return jnp.where(iota((rows, cols), 1) == target(iota((rows, 1), 0)), 1.0, 0.0).astype(BF)


def pack_at(row):
    p, s, th, k = row >> 8, (row >> 3) & 31, (row >> 1) & 3, row & 1
    return th * LANES + HALF * p + K2 * s + k


def spread_at(row):
    s, ri, j2, k = row >> 3, (row >> 2) & 1, (row >> 1) & 1, row & 1
    j = 2 * s + j2
    return ri * ROWS + k * SLOTS + jnp.where(s < S // 2, j, 2 * S - j)


def order_at(row):
    s, rj, k = row >> 3, (row >> 1) & 3, row & 1
    return rj * HALF + K2 * s + k


def unpack_at(row):
    s, p, h, k = row >> 3, (row >> 2) & 1, (row >> 1) & 1, row & 1
    return h * LANES + HALF * p + K2 * s + k


def make_forward_outer():
    slot = iota((SLOTS, S), 0)
    used = jnp.where(slot <= S, 1.0, 0.0)
    angle = ((slot * iota((SLOTS, S), 1)) & (2 * S - 1)).astype(F32) * (math.pi / S)
    high, low = split(jnp.concatenate([jnp.cos(angle) * used, -jnp.sin(angle) * used], axis=0))
    return jnp.concatenate([high, low], axis=1)


def make_inverse_outer():
    slot = iota((S, SLOTS), 1)
    used = jnp.where(slot <= S, 1.0 / N, 0.0)
    angle = ((slot * iota((S, SLOTS), 0)) & (2 * S - 1)).astype(F32) * (math.pi / S)
    high, low = split(jnp.concatenate([jnp.cos(angle) * used, -jnp.sin(angle) * used], axis=1))
    return jnp.concatenate([high, low, high], axis=1)


def make_twist(ref):
    angle = (iota((SLOTS, C), 0) * iota((SLOTS, C), 1)).astype(F32) * (2 * math.pi / N)
    ref[0] = jnp.cos(angle)
    ref[1] = jnp.sin(angle)


def make_inner(high_ref, low_ref):
    angle = ((iota((C, C), 0) * iota((C, C), 1)) & (C - 1)).astype(F32) * (2 * math.pi / C)
    for x, places in ((jnp.cos(angle), ((0, 0, 1), (1, 1, 1))), (jnp.sin(angle), ((1, 0, 1), (0, 1, -1)))):
        high, low = split(x)
        for i, j, sign in places:
            at = (pl.ds(C * i, C), pl.ds(C * j, C))
            high_ref[at] = high if sign > 0 else -high
            low_ref[at] = low if sign > 0 else -low


CONSTANTS = dict(
    pack=((512, 512), BF),
    fo=((2 * SLOTS, 2 * S), BF),
    wh=((2 * C, 2 * C), BF),
    wl=((2 * C, 2 * C), BF),
    tw=((2, SLOTS, C), F32),
    spread=((256, 2 * ROWS), BF),
    order_t=((256, 256), BF),
    order=((256, 256), BF),
    spread_t=((2 * ROWS, 256), BF),
    io=((S, 6 * SLOTS), BF),
    unpack=((256, 256), BF),
)


def dot(x, y):
    return lax.dot_general(x, y, (((1,), (0,)), ((), ())), preferred_element_type=F32)


def dot_t(x, y):
    return lax.dot_general(x, y, (((1,), (1,)), ((), ())), preferred_element_type=F32)


def split(x):
    high = x.astype(BF)
    return high, (x - high.astype(F32)).astype(BF)


def pack_block(x, g, pack):
    cols = jnp.concatenate([x[:LANES], x[LANES:], g[:LANES], g[LANES:]], axis=1)
    return dot_t(pack, cols).reshape(S, 8, LANES).astype(BF)


def forward(d, fo, tc, ts, wh, wl):
    dt = jnp.swapaxes(d, 0, 1).astype(BF)
    cols = [dt[8 * q + 4 * t + 2 * h + k] for t in range(2) for q in range(2) for k in range(K2) for h in range(2)]
    dc = jnp.concatenate(cols, axis=1)
    z = dot(fo, jnp.concatenate([dc, dc], axis=0))
    re, im = [], []
    for i in range(4 * K2):
        zr = z[:SLOTS, C * i : C * i + C]
        zi = z[SLOTS:, C * i : C * i + C]
        re.append(zr * tc + zi * ts)
        im.append(zi * tc - zr * ts)
    rows = jnp.concatenate([jnp.concatenate(re, axis=0), jnp.concatenate(im, axis=0)], axis=1)
    high, low = split(rows)
    out = dot(high, wh) + dot(low, wh) + dot(high, wl)
    return out[: 2 * ROWS], out[2 * ROWS :]


def product(x, g):
    xr, xi, gr, gi = x[:, :C], x[:, C:], g[:, :C], g[:, C:]
    both = jnp.concatenate([xr * gr + xi * gi, xr * gi - xi * gr], axis=1)
    return both[:ROWS] + both[ROWS:]


def spread_grad(total, spread):
    cols = jnp.concatenate([total[:, :C], total[:, C:]], axis=0) * (1.0 / N)
    return dot(spread, cols.astype(BF))


def turn(flip):
    row = lax.broadcasted_iota(jnp.int32, (C, C), 0)
    col = lax.broadcasted_iota(jnp.int32, (C, C), 1)
    return jnp.where(col == jnp.where(flip, C - 1 - row, row), 1.0, 0.0).astype(BF)


def own_grad(cols, order_t, r):
    return dot_t(r, dot(order_t, cols).astype(BF))


def spread_filter(k, order, r):
    return dot_t(order, dot(r, k.astype(BF)).astype(BF))


def inverse(x, kr, ki, io, tc, ts, wh, wl):
    xr, xi = x[:, :C], x[:, C:]
    kr, ki = jnp.concatenate([kr, kr], axis=0), jnp.concatenate([ki, ki], axis=0)
    mixed = jnp.concatenate([xr * kr - xi * ki, xr * ki + xi * kr], axis=1).astype(BF)
    o = dot_t(mixed, wh) + dot_t(mixed, wl)
    cols = []
    for i in range(2 * K2):
        zr = o[SLOTS * i : SLOTS * (i + 1), :C]
        zi = o[SLOTS * i : SLOTS * (i + 1), C:]
        cols.append(jnp.concatenate([zr * tc - zi * ts, zr * ts + zi * tc], axis=0))
    vh, vl = split(jnp.concatenate(cols, axis=1))
    y = dot(io, jnp.concatenate([vh, vh, vl], axis=0))
    parts = [
        y[:, C * (K2 * q + k) + LANES * h : C * (K2 * q + k) + LANES * (h + 1)]
        for q in range(2)
        for h in range(2)
        for k in range(K2)
    ]
    return jnp.swapaxes(jnp.stack(parts, axis=0), 0, 1)


def unpack_block(y, unpack):
    row = lax.broadcasted_iota(jnp.int32, (LANES, LANES), 0)
    col = lax.broadcasted_iota(jnp.int32, (LANES, LANES), 1)
    eye = jnp.where(row == col, 1.0, 0.0).astype(BF)
    return dot(dot_t(eye, y).astype(BF), unpack).astype(BF)


def cross(x0, x1):
    first = lax.broadcasted_iota(jnp.int32, x0.shape, 1) < HALF
    return (
        jnp.where(first, x0, pltpu.roll(x1, HALF, axis=1)),
        jnp.where(first, pltpu.roll(x0, HALF, axis=1), x1),
    )


def kernel(
    x_hbm, g_hbm, k_hbm, f_hbm, s_hbm, *rest
):
    nk_hbm, nf_hbm, ns_hbm, y_hbm = rest[:4]
    rest = rest[4:]
    consts = dict(zip(CONSTANTS, rest[: len(CONSTANTS)]))
    (
        x_v, g_v, k_v, f_v, s_v, y_v,
        packed, xs, xr, spec, total, gs, gr, ks, kr, kc, ys, yr,
        group_sem, in_sem, state_sem, out_sem,
        xs_sem, xr_sem, gs_sem, gr_sem, ks_sem, kr_sem, ys_sem, yr_sem,
    ) = rest[len(CONSTANTS) :]
    me = lax.axis_index("seq")
    mb = lax.axis_index("batch")

    barrier = pltpu.get_barrier_semaphore()

    def greet_seq(e, carry):
        pl.semaphore_signal(
            barrier, inc=1, device_id={"seq": lax.rem(me + e, S), "batch": mb}, device_id_type=pl.DeviceIdType.MESH
        )
        return carry

    def greet_batch(d, carry):
        pl.semaphore_signal(
            barrier, inc=1, device_id={"seq": me, "batch": lax.rem(mb + d, B)}, device_id_type=pl.DeviceIdType.MESH
        )
        return carry

    def greet_groups(d, carry):
        pl.semaphore_signal(
            group_sem.at[mb],
            inc=1,
            device_id={"seq": me, "batch": lax.rem(mb + d, B)},
            device_id_type=pl.DeviceIdType.MESH,
        )
        return carry

    lax.fori_loop(1, S, greet_seq, 0, unroll=S - 1)
    lax.fori_loop(1, B, greet_batch, 0, unroll=B - 1)

    loads = [
        pltpu.make_async_copy(x_hbm, x_v, in_sem.at[0]),
        pltpu.make_async_copy(g_hbm, g_v, in_sem.at[1]),
    ]
    state_loads = [
        pltpu.make_async_copy(k_hbm, k_v, state_sem.at[0]),
        pltpu.make_async_copy(f_hbm, f_v, state_sem.at[1]),
        pltpu.make_async_copy(s_hbm, s_v, state_sem.at[2]),
    ]
    for copy in loads + state_loads:
        copy.start()
    consts["pack"][...] = selection(512, 512, pack_at)
    for copy in loads:
        copy.wait()

    def pack(p, to):
        cols = pl.ds(pl.multiple_of(to * LANES, LANES), LANES)
        rows = pl.ds(256 * p, 256)
        xs[p, to] = pack_block(x_v[:, cols], g_v[:, cols], consts["pack"][rows])

    pack(0, mb)
    pl.semaphore_wait(barrier, S - 1 + B - 1)
    lax.fori_loop(1, B, greet_groups, 0, unroll=B - 1)

    def send_block(p, d, first):
        to = lax.rem(mb + d, B)
        if p == 1 or first == 0:
            pack(p, to)
        if p == 0 and first == 0:
            pl.semaphore_wait(group_sem.at[to], 1)

        def one(e, carry):
            there = lax.rem(me + e, S)
            pltpu.make_async_remote_copy(
                src_ref=xs.at[p, to, there],
                dst_ref=xr.at[p, mb, me],
                send_sem=xs_sem.at[p, d],
                recv_sem=xr_sem.at[p, mb],
                device_id={"seq": there, "batch": to},
                device_id_type=pl.DeviceIdType.MESH,
            ).start()
            return carry

        lax.fori_loop(first, S, one, 0, unroll=8 if first == 0 else 1)

    def send_own(p):
        send_block(p, 0, 1)
        pltpu.make_async_copy(xs.at[p, mb, me], xr.at[p, mb, me], xr_sem.at[p, mb]).start()

    def send_blocks(p, start, stop):
        def step(d, carry):
            send_block(p, d, 0)
            return carry

        lax.fori_loop(start, stop, step, 0)

    send_own(0)
    send_own(1)
    send_blocks(0, 1, B)
    send_blocks(1, 1, B)
    consts["fo"][...] = make_forward_outer()
    make_twist(consts["tw"])
    make_inner(consts["wh"], consts["wl"])
    consts["spread"][...] = selection(256, 2 * ROWS, spread_at)
    consts["spread_t"][...] = selection(256, 2 * ROWS, spread_at, True)
    consts["order"][...] = selection(256, 256, order_at)
    consts["order_t"][...] = selection(256, 256, order_at, True)
    consts["io"][...] = make_inverse_outer()
    consts["unpack"][...] = selection(256, 256, unpack_at)
    for copy in state_loads:
        copy.wait()
    for i, ref in enumerate((k_v, f_v, s_v)):
        for ri in range(2):
            packed[i, 0, ri], packed[i, 1, ri] = cross(ref[ri, 0], ref[ri, 1])
    total[...] = jnp.zeros_like(total)

    def pair(i):
        return [lax.rem(mb + B - 2 * i - q, B) for q in range(2)]

    def forward_pair(p, i):
        for q in pair(i):
            pltpu.make_async_copy(xr.at[p, q], xr.at[p, q], xr_sem.at[p, q]).wait()
        sx, sg = forward(
            jnp.concatenate([xr[p, q].astype(F32) for q in pair(i)], axis=1),
            consts["fo"][...],
            consts["tw"][0],
            consts["tw"][1],
            consts["wh"][...],
            consts["wl"][...],
        )
        spec[p, i] = sx
        total[p] += product(sx, sg)

    def forward_pairs(p, start, stop):
        def step(i, carry):
            forward_pair(p, i)
            return carry

        lax.fori_loop(start, stop, step, 0)

    def exchange(sent, landed, send_sem, recv_sem):
        pltpu.make_async_copy(sent.at[me], landed.at[me], recv_sem).start()

        def one(e, carry):
            there = lax.rem(me + e, S)
            pltpu.make_async_remote_copy(
                src_ref=sent.at[there],
                dst_ref=landed.at[me],
                send_sem=send_sem,
                recv_sem=recv_sem,
                device_id={"seq": there, "batch": mb},
                device_id_type=pl.DeviceIdType.MESH,
            ).start()
            return carry

        lax.fori_loop(1, S, one, 0)

    def store_halves(ref, value):
        for h in range(2):
            ref[:, h] = value[:, LANES * h : LANES * (h + 1)].reshape(S, 8, LANES).astype(BF)

    def halves(ref):
        return jnp.concatenate(
            [ref[:, h].astype(F32).reshape(S * 8, LANES).astype(BF) for h in range(2)], axis=1
        )

    def send_grad(p):
        store_halves(gs.at[p], spread_grad(total[p], consts["spread"][...]))
        exchange(gs.at[p], gr.at[p], gs_sem.at[p], gr_sem.at[p])

    flip = me >= S // 2
    sign = jnp.where(flip, -1.0, 1.0).astype(F32)

    def update(p):
        r = turn(flip)
        pltpu.make_async_copy(gr.at[p], gr.at[p], gr_sem.at[p]).wait()
        grad = own_grad(halves(gr.at[p]), consts["order_t"][...], r)
        cols = []
        for ri in range(2):
            part = grad[:, LANES * ri : LANES * (ri + 1)]
            if ri == 1:
                part = part * sign
            first = 0.9 * packed[1, p, ri] + 0.1 * part
            second = 0.99 * packed[2, p, ri] + 0.01 * part * part
            new = packed[0, p, ri] - 0.5 * jnp.tanh(first / (jnp.sqrt(second) + 1e-6))
            packed[0, p, ri] = new
            packed[1, p, ri] = first
            packed[2, p, ri] = second
            cols.append(new * sign if ri == 1 else new)
        store_halves(ks.at[p], spread_filter(jnp.concatenate(cols, axis=1), consts["order"][...], r))
        exchange(ks.at[p], kr.at[p], ks_sem.at[p], kr_sem.at[p])

    def inverse_pair(p, i, own):
        y = inverse(
            spec[p, i], kc[p, :ROWS], kc[p, ROWS:], consts["io"][...], consts["tw"][0], consts["tw"][1],
            consts["wh"][...], consts["wl"][...],
        )
        for part, q in enumerate(pair(i)):
            ys[p, q] = y[:, 4 * part : 4 * part + 4].astype(BF)

            def one(e, carry):
                there = lax.rem(me + e, S)
                pltpu.make_async_remote_copy(
                    src_ref=ys.at[p, q, there],
                    dst_ref=yr.at[p, mb, me],
                    send_sem=ys_sem.at[p, q],
                    recv_sem=yr_sem.at[p, mb],
                    device_id={"seq": there, "batch": q},
                    device_id_type=pl.DeviceIdType.MESH,
                ).start()
                return carry

            lax.fori_loop(1 if own and part == 0 else 0, S, one, 0, unroll=1 if own and part == 0 else 8)

    def inverse_start(p):
        pltpu.make_async_copy(kr.at[p], kr.at[p], kr_sem.at[p]).wait()
        kc[p] = dot(consts["spread_t"][...], halves(kr.at[p]))
        inverse_pair(p, 0, True)
        pltpu.make_async_copy(ys.at[p, mb, me], yr.at[p, mb, me], yr_sem.at[p, mb]).start()

    def inverse_pairs(p, start, stop):
        def step(i, carry):
            inverse_pair(p, i, False)
            return carry

        lax.fori_loop(start, stop, step, 0)

    forward_pairs(0, 0, 4)
    send_grad(0)
    forward_pairs(1, 0, 4)
    send_grad(1)
    update(0)
    update(1)
    for i, ref in enumerate((k_v, f_v, s_v)):
        for ri in range(2):
            ref[ri, 0], ref[ri, 1] = cross(packed[i, 0, ri], packed[i, 1, ri])
    stores = [
        pltpu.make_async_copy(k_v, nk_hbm, out_sem.at[0]),
        pltpu.make_async_copy(f_v, nf_hbm, out_sem.at[1]),
        pltpu.make_async_copy(s_v, ns_hbm, out_sem.at[2]),
    ]
    for copy in stores:
        copy.start()
    inverse_start(0)
    inverse_pairs(0, 1, B // 2)
    inverse_start(1)
    inverse_pairs(1, 1, B // 2)

    def finish_step(d, carry):
        came = lax.rem(mb + d, B)
        for p in range(2):
            pltpu.make_async_copy(yr.at[p, came], yr.at[p, came], yr_sem.at[p, came]).wait()
        rows = jnp.concatenate([yr[p, came].astype(F32) for p in range(2)], axis=1)
        o = unpack_block(rows.reshape(S * 8, LANES).astype(BF), consts["unpack"][...])
        at = pl.ds(pl.multiple_of(came * LANES, LANES), LANES)
        y_v[:LANES, at] = o[:, :LANES]
        y_v[LANES:, at] = o[:, LANES:]
        pltpu.make_async_copy(y_v.at[:, at], y_hbm.at[:, at], out_sem.at[3]).start()
        return carry

    lax.fori_loop(0, B, finish_step, 0)

    for p in range(2):

        def drain(d, carry):
            other = lax.rem(mb + d, B)
            pltpu.make_async_copy(xs.at[p, 0], xs.at[p, 0], xs_sem.at[p, d]).wait()
            pltpu.make_async_copy(ys.at[p, 0], ys.at[p, 0], ys_sem.at[p, other]).wait()
            return carry

        for buffer, sem in (
            (xs.at[p, 0], xs_sem.at[p, 0]),
            (gs.at[p], gs_sem.at[p]),
            (ks.at[p], ks_sem.at[p]),
            (ys.at[p, 0], ys_sem.at[p, mb]),
        ):
            part = buffer.at[pl.ds(0, S - 1)]
            pltpu.make_async_copy(part, part, sem).wait()
        lax.fori_loop(1, B, drain, 0)
    for copy in stores:
        copy.wait()
    pltpu.make_async_copy(y_v, y_hbm, out_sem.at[3]).wait()


def hand_over(*refs):
    sems = refs[8]
    copies = []
    for i in range(4):
        count = 2 if i < 3 else 4
        size = refs[i].shape[0] // count
        for j in range(count):
            part = pl.ds(j * size, size)
            copies.append(pltpu.make_async_copy(refs[i].at[part], refs[4 + i].at[part], sems.at[i, j]))
    for copy in copies:
        copy.start()
    for copy in copies:
        copy.wait()


def per_device(inputs, grad_out, spectrum, first_moment, second_moment):
    any_spec = pl.BlockSpec(memory_space=pl.ANY)
    hbm_spec = pl.BlockSpec(memory_space=pltpu.HBM)
    state = (2, 2, C, LANES)
    wide = (C, B * LANES)
    dma = pltpu.SemaphoreType.DMA
    scratch = [pltpu.VMEM(shape, dtype) for shape, dtype in CONSTANTS.values()]
    scratch += [
        pltpu.VMEM(wide, BF),
        pltpu.VMEM(wide, BF),
        pltpu.VMEM(state, F32),
        pltpu.VMEM(state, F32),
        pltpu.VMEM(state, F32),
        pltpu.VMEM(wide, BF),
        pltpu.VMEM((3, 2, 2, C, LANES), F32),
        pltpu.VMEM((2, B, S, 8, LANES), BF),
        pltpu.VMEM((2, B, S, 8, LANES), BF),
        pltpu.VMEM((2, B // 2, 2 * ROWS, 2 * C), F32),
        pltpu.VMEM((2, ROWS, 2 * C), F32),
        pltpu.VMEM((2, S, 2, 8, LANES), BF),
        pltpu.VMEM((2, S, 2, 8, LANES), BF),
        pltpu.VMEM((2, S, 2, 8, LANES), BF),
        pltpu.VMEM((2, S, 2, 8, LANES), BF),
        pltpu.VMEM((2, 2 * ROWS, C), F32),
        pltpu.VMEM((2, B, S, 4, LANES), BF),
        pltpu.VMEM((2, B, S, 4, LANES), BF),
        pltpu.SemaphoreType.REGULAR((B,)),
        dma((2,)),
        dma((3,)),
        dma((4,)),
        dma((2, B)),
        dma((2, B)),
        dma((2,)),
        dma((2,)),
        dma((2,)),
        dma((2,)),
        dma((2, B)),
        dma((2, B)),
    ]
    results = pl.pallas_call(
        kernel,
        out_shape=(
            jax.ShapeDtypeStruct(state, F32),
            jax.ShapeDtypeStruct(state, F32),
            jax.ShapeDtypeStruct(state, F32),
            jax.ShapeDtypeStruct(wide, BF),
        ),
        in_specs=[hbm_spec] * 5,
        out_specs=(any_spec,) * 4,
        scratch_shapes=scratch,
        compiler_params=pltpu.CompilerParams(
            collective_id=0, has_side_effects=True, vmem_limit_bytes=48 * 1024 * 1024
        ),
        name="long_convolution_update",
    )(*[pltpu.with_memory_space_constraint(x, pltpu.HBM) for x in (inputs[0], grad_out[0], spectrum, first_moment, second_moment)])
    nk, nf, ns, y = pl.pallas_call(
        hand_over,
        out_shape=[jax.ShapeDtypeStruct(x.shape, x.dtype) for x in results],
        in_specs=[any_spec] * 4,
        out_specs=[hbm_spec] * 4,
        scratch_shapes=[dma((4, 4))],
        compiler_params=pltpu.CompilerParams(vmem_limit_bytes=1024 * 1024),
        name="hand_over",
    )(*results)
    return nk, nf, ns, y[None]


def solution(mesh):
    state = P(None, "seq", None, "batch")
    rows = P("batch", "seq", None)
    return jax.shard_map(
        per_device,
        mesh=mesh,
        in_specs=(rows, rows, state, state, state),
        out_specs=(state, state, state, rows),
        check_vma=False,
    )
```
